32 devices in a mesh: view: 2 (over x), fx: 4 (over y, core), fy: 4 (over z).
Axes of the slice: x: 2, y: 2, z: 4, core: 2. Of those that a mesh axis runs over, the one named last changes fastest.
Arguments:
- estimate: float32 [128, 128, 128], P('fx', 'fy'), may hold values from 0.25 to 30
- images: bfloat16 [6, 128, 128, 128], P('view', 'fx', 'fy'), may hold values from 0.1 to 30
- psf: float32 [6, 3, 31], P('view'), may hold values from 0.05 to 1
- cover_lo: int32 [6, 4, 4], P('view'), may hold values from 0 to 63
- cover_len: int32 [6, 4, 4], P('view'), may hold values from 32 to 64
Outputs:
- joined: float32 [128, 128, 128], P('fx', 'fy')
The draws below stay inside these ranges and needn't reach their ends.
All inputs are finite; a program needn't handle non-finite values.
Results may differ from the reference program's by a relative error of at most 0.0003.
Values may be sent and summed in bfloat16 or wider, within the bound.
No kernel may reach another device: no remote copies, remote signals or barrier semaphores. Data moves between devices by JAX's collectives and lax.ppermute only.
A program may use at most 64 MiB of HBM per device.

```python
import math
import jax
import jax.numpy as jnp
from jax import lax

CX = 32
CY = 32
NZ = 128
VIEWS = 6
TAPS = 31
ITERS = 2
GX = 4
GY = 4
NX = 128
NY = 128


def smooth_part(subkey, strength):
    phases = jax.random.uniform(subkey, (2, 3), jnp.float32)
    cycles = 1.0 + phases[0]
    pos_x = jnp.arange(NX, dtype=jnp.float32) / NX
    pos_y = jnp.arange(NY, dtype=jnp.float32) / NY
    pos_z = jnp.arange(NZ, dtype=jnp.float32) / NZ
    wave_x = jnp.cos(2.0 * math.pi * (cycles[0] * pos_x + phases[1, 0]))
    wave_y = jnp.cos(2.0 * math.pi * (cycles[1] * pos_y + phases[1, 1]))
    wave_z = jnp.cos(2.0 * math.pi * (cycles[2] * pos_z + phases[1, 2]))
    summed = wave_x[:, None, None] + wave_y[None, :, None] + wave_z[None, None, :]
    return jnp.exp(strength * summed)


def expand_cells(table, cell_side):
    grown = jnp.repeat(jnp.repeat(jnp.repeat(table, cell_side, axis=0), cell_side, axis=1), cell_side, axis=2)
    return grown[:NX, :NY, :NZ]


def blob_part(subkey, bright_lo, bright_hi):
    cell_side = 16
    cell_counts = ((NX + cell_side - 1) // cell_side, (NY + cell_side - 1) // cell_side, (NZ + cell_side - 1) // cell_side)
    subkeys = jax.random.split(subkey, 4)
    centres = jax.random.uniform(subkeys[0], cell_counts + (3,), jnp.float32, 5.0, 11.0)
    radius = jnp.exp(jax.random.uniform(subkeys[1], cell_counts, jnp.float32, 0.0, math.log(3.0)))
    bright = jnp.exp(jax.random.uniform(subkeys[2], cell_counts, jnp.float32, math.log(bright_lo), math.log(bright_hi)))
    lit_cells = jax.random.bernoulli(subkeys[3], 0.5, cell_counts)
    levels = jnp.where(lit_cells, bright, jnp.zeros_like(bright))
    offset_x = (jnp.arange(NX, dtype=jnp.int32) % cell_side).astype(jnp.float32)
    offset_y = (jnp.arange(NY, dtype=jnp.int32) % cell_side).astype(jnp.float32)
    offset_z = (jnp.arange(NZ, dtype=jnp.int32) % cell_side).astype(jnp.float32)
    dist_sq = (offset_x[:, None, None] - expand_cells(centres[..., 0], cell_side)) ** 2
    dist_sq = dist_sq + (offset_y[None, :, None] - expand_cells(centres[..., 1], cell_side)) ** 2
    dist_sq = dist_sq + (offset_z[None, None, :] - expand_cells(centres[..., 2], cell_side)) ** 2
    spread = expand_cells(radius, cell_side)
    return expand_cells(levels, cell_side) * jnp.exp(-dist_sq / (2.0 * spread * spread))


def structured_volume(subkey, noise_lo, noise_hi):
    subkeys = jax.random.split(subkey, 3)
    smooth = smooth_part(subkeys[0], 0.12)
    noise = jnp.exp(jax.random.uniform(subkeys[1], (NX, NY, NZ), jnp.float32, math.log(noise_lo), math.log(noise_hi)))
    blobs = blob_part(subkeys[2], 3.0, 10.0)
    return smooth * (noise + blobs)


def draw_estimate(key, part):
    return structured_volume(jax.random.fold_in(key, 11), 0.5, 2.0)


def draw_images(key, part):
    view_keys = jax.random.split(jax.random.fold_in(key, 23), VIEWS)

    def one_view(view_key):
        return structured_volume(view_key, 0.25, 4.0).astype(jnp.bfloat16)
    return jax.lax.map(one_view, view_keys)


def place_ends(result, rng, least, top_value):
    index_at = [jax.random.randint(jax.random.fold_in(rng, axis), (), 0, length) for axis, length in enumerate(result.shape)]
    longest = result.shape.index(max(result.shape))
    next_to = index_at[:longest] + [(index_at[longest] + 1) % result.shape[longest]] + index_at[longest + 1:]
    return result.at[tuple(index_at)].set(least).at[tuple(next_to)].set(top_value)


def level_of(rng, shape, pieces, least, largest):
    loudness = 1.0
    for position, blocks in pieces:
        draws = jax.random.uniform(jax.random.fold_in(jax.random.fold_in(rng, 6), position), (blocks,), jnp.float32, least / len(pieces), largest / len(pieces))
        loudness = loudness * jnp.repeat(jnp.exp(draws), shape[position] // blocks).reshape((-1,) + (1,) * (len(shape) - 1 - position))
    return loudness


def setup_inputs(seed: int = 0) -> dict:
    streams_of = jax.random.split(jax.random.key(seed), 6)
    return {
        "estimate": draw_estimate(jax.random.fold_in(streams_of[5], 71), 0),
        "images": draw_images(jax.random.fold_in(streams_of[5], 71), 0),
        "psf": jnp.clip(jnp.exp(math.log(1.0) - 2.9957323 * jax.random.uniform(streams_of[2], (VIEWS, 3, TAPS), jnp.float32) ** level_of(streams_of[2], (VIEWS, 3, TAPS), ((0, 2),), -0.2, 0.2)), 0.05, 1.0),
        "cover_lo": place_ends(jax.random.randint(streams_of[3], (VIEWS, GX, GY), 0, NZ // 2), jax.random.fold_in(streams_of[3], 1), 0, (NZ // 2) - 1).astype(jnp.int32),
        "cover_len": place_ends(jax.random.randint(streams_of[4], (VIEWS, GX, GY), NZ // 4, NZ // 2 + 1), jax.random.fold_in(streams_of[4], 1), NZ // 4, (NZ // 2 + 1) - 1).astype(jnp.int32),
    }


def blur_axis(field, weights, axis, backward):
    taps = weights.shape[0]
    radius = (taps - 1) // 2
    widths = [(0, 0), (0, 0), (0, 0)]
    widths[axis] = (radius, radius)
    padded = jnp.pad(field, widths)
    length = field.shape[axis]
    total = jnp.zeros(field.shape, jnp.float32)
    for tap in range(taps):
        start = taps - 1 - tap if backward else tap
        total = total + weights[tap] * lax.slice_in_dim(padded, start, start + length, axis=axis)
    return total


def blur_all(field, weights, backward):
    for axis in range(3):
        field = blur_axis(field, weights[axis], axis, backward)
    return field


def reference(estimate, images, psf, cover_lo, cover_len):
    kern = psf / jnp.sum(psf, axis=-1, keepdims=True)
    depth = jnp.arange(NZ, dtype=jnp.int32)
    masked = []
    weight = jnp.zeros(estimate.shape, jnp.float32)
    for view in range(VIEWS):
        low = jnp.repeat(jnp.repeat(cover_lo[view], CX, axis=0), CY, axis=1)
        span = jnp.repeat(jnp.repeat(cover_len[view], CX, axis=0), CY, axis=1)
        inside = (depth >= low[:, :, None]) & (depth < (low + span)[:, :, None])
        weight = weight + blur_all(inside.astype(jnp.float32), kern[view], True)
        masked.append(jnp.where(inside, images[view], jnp.zeros_like(images[view])))
    joined = estimate
    for step in range(ITERS):
        correction = jnp.zeros(estimate.shape, jnp.float32)
        for view in range(VIEWS):
            blurred = blur_all(joined, kern[view], False)
            ratio = masked[view].astype(jnp.float32) / blurred
            correction = correction + blur_all(ratio, kern[view], True)
        joined = joined * (correction + 0.5) / (weight + 0.5)
    return joined
```

```python
import jax
import jax.numpy as jnp
from jax import lax
from jax.sharding import PartitionSpec as P

ITERS = 2


def shift_pairs(peers):
    up = [(i, i + 1) for i in range(peers - 1)]
    return up, [(j, i) for i, j in up]


def gather_halo(array, axis, dim, width):
    up, down = shift_pairs(lax.axis_size(axis))
    length = array.shape[dim]
    last = lax.slice_in_dim(array, length - width, length, axis=dim)
    first = lax.slice_in_dim(array, 0, width, axis=dim)
    before = lax.ppermute(last, axis, up)
    after = lax.ppermute(first, axis, down)
    return jnp.concatenate([before, array, after], axis=dim)


def scatter_halo(array, axis, dim, width):
    up, down = shift_pairs(lax.axis_size(axis))
    length = array.shape[dim]
    head = lax.ppermute(lax.slice_in_dim(array, 0, width, axis=dim), axis, down)
    tail = lax.ppermute(lax.slice_in_dim(array, length - width, length, axis=dim), axis, up)
    centre = lax.slice_in_dim(array, width, length - width, axis=dim)
    inner = [(0, 0, 0)] * array.ndim
    inner[dim] = (0, length - 3 * width, 0)
    outer = [(0, 0, 0)] * array.ndim
    outer[dim] = (length - 3 * width, 0, 0)
    zero = jnp.zeros((), array.dtype)
    return centre + lax.pad(tail, zero, inner) + lax.pad(head, zero, outer)


def band(weights, rows, cols, shift):
    taps = weights.shape[-1]
    gap = (
        jnp.arange(cols, dtype=jnp.int32)[None, :]
        - jnp.arange(rows, dtype=jnp.int32)[:, None]
        + shift
    )
    picks = (gap[:, :, None] == jnp.arange(taps, dtype=jnp.int32)).astype(jnp.float32)
    return jnp.einsum("oit,gt->goi", picks, weights, precision=lax.Precision.HIGHEST)


def block_sums(weights, axis, cells):
    blocks = lax.axis_size(axis)
    taps = weights.shape[-1]
    place = lax.axis_index(axis) * cells + jnp.arange(cells, dtype=jnp.int32)
    source = place[:, None] - jnp.arange(taps, dtype=jnp.int32)[None, :] + (taps - 1) // 2
    first = jnp.arange(blocks, dtype=jnp.int32)[:, None, None] * cells
    picks = ((source[None] >= first) & (source[None] < first + cells)).astype(jnp.float32)
    return jnp.einsum("bot,gt->ogb", picks, weights, precision=lax.Precision.HIGHEST)


def weight_of(kern, low, span, cells_x, cells_y, depth):
    views = kern.shape[0]
    taps = kern.shape[-1]
    sums_x = block_sums(kern[:, 0], "fx", cells_x)
    sums_y = block_sums(kern[:, 1], "fy", cells_y)
    levels = jnp.arange(depth, dtype=jnp.int32)
    inside = (levels >= low[..., None]) & (levels < (low + span)[..., None])
    table_z = band(kern[:, 2], depth, depth, (taps - 1) // 2)
    sums_z = jnp.einsum(
        "gxyi,gio->gxyo", inside.astype(jnp.float32), table_z, precision=lax.Precision.HIGHEST
    )
    plane = sums_x[:, None, :, :, None] * sums_y[None, :, :, None, :]
    plane = plane.reshape(cells_x, cells_y, -1)
    return jnp.einsum(
        "xym,mz->xyz", plane, sums_z.reshape(-1, depth), precision=lax.Precision.HIGHEST
    )


def body(estimate, images, psf, cover_lo, cover_len):
    group, cells_x, cells_y, depth = images.shape
    taps = psf.shape[-1]
    radius = (taps - 1) // 2
    halo = min(-(-radius // 16) * 16, cells_x, cells_y)
    exact = lax.Precision.HIGH
    groups = lax.axis_size("view")
    swap = [(i, (i + 1) % groups) for i in range(groups)]

    kern = psf / jnp.sum(psf, axis=-1, keepdims=True)
    pack = jnp.concatenate(
        [kern.reshape(-1), cover_lo.reshape(-1).astype(jnp.float32), cover_len.reshape(-1).astype(jnp.float32)]
    )
    packs = [pack]
    for _ in range(groups - 1):
        packs.append(lax.ppermute(packs[-1], "view", swap))
    packs = jnp.stack(packs)
    all_kern = packs[:, : kern.size].reshape((-1,) + kern.shape[1:])
    cells = cover_lo.size
    all_low = packs[:, kern.size : kern.size + cells].astype(jnp.int32).reshape((-1,) + cover_lo.shape[1:])
    all_span = packs[:, kern.size + cells :].astype(jnp.int32).reshape((-1,) + cover_len.shape[1:])
    lower_part = weight_of(all_kern, all_low, all_span, cells_x, cells_y, depth) + 0.5

    block_x, block_y = lax.axis_index("fx"), lax.axis_index("fy")
    low = lax.dynamic_slice(cover_lo, (0, block_x, block_y), (group, 1, 1))[..., None]
    span = lax.dynamic_slice(cover_len, (0, block_x, block_y), (group, 1, 1))[..., None]
    levels = jnp.arange(depth, dtype=jnp.int32)
    own = (levels >= low) & (levels < low + span)
    masked = jnp.where(own, images, jnp.zeros_like(images)).astype(jnp.float32)

    table_x = band(kern[:, 0], cells_x, cells_x + 2 * halo, radius - halo)
    table_y = band(kern[:, 1], cells_y, cells_y + 2 * halo, radius - halo)
    table_z = band(kern[:, 2], depth, depth, radius)

    joined = estimate
    for step in range(ITERS):
        wide = gather_halo(joined.astype(jnp.bfloat16), "fy", 1, halo)
        wide = gather_halo(wide, "fx", 0, halo).astype(jnp.float32)
        field = jnp.einsum("gox,xyz->goyz", table_x, wide, precision=exact)
        field = jnp.einsum("goy,gxyz->gxoz", table_y, field, precision=exact)
        blurred = jnp.einsum("goz,gxyz->gxyo", table_z, field, precision=exact)
        ratio = masked / blurred
        field = jnp.einsum("goz,gxyo->gxyz", table_z, ratio, precision=exact)
        field = jnp.einsum("goy,gxoz->gxyz", table_y, field, precision=exact)
        field = jnp.einsum("gox,goyz->xyz", table_x, field, precision=exact)
        field = scatter_halo(field, "fx", 0, halo)
        field = scatter_halo(field, "fy", 1, halo)
        correction = field
        moving = field
        for _ in range(groups - 1):
            moving = lax.ppermute(moving, "view", swap)
            correction = correction + moving
        joined = joined * (correction + 0.5) / lower_part
    return joined


def solution(mesh):
    return jax.shard_map(
        body,
        mesh=mesh,
        in_specs=(
            P("fx", "fy", None),
            P("view", "fx", "fy", None),
            P("view", None, None),
            P("view", None, None),
            P("view", None, None),
        ),
        out_specs=P("fx", "fy", None),
        check_vma=False,
    )
```

```python
import jax
import jax.numpy as jnp
from jax import lax
from jax.sharding import PartitionSpec as P

ITERS = 2


def swap_edges(to_below, to_above, axis):
    peers = lax.axis_size(axis)
    even = lax.axis_index(axis) % 2 == 0

    def pairs(start):
        out = []
        for i in range(start, peers - 1, 2):
            out += [(i, i + 1), (i + 1, i)]
        return out

    first = lax.ppermute(jnp.where(even, to_above, to_below), axis, pairs(0))
    second = lax.ppermute(jnp.where(even, to_below, to_above), axis, pairs(1))
    return jnp.where(even, second, first), jnp.where(even, first, second)


def gather_halo(array, axis, dim, width):
    length = array.shape[dim]
    before, after = swap_edges(
        lax.slice_in_dim(array, 0, width, axis=dim),
        lax.slice_in_dim(array, length - width, length, axis=dim),
        axis,
    )
    return jnp.concatenate([before, array, after], axis=dim)


def add_edges(centre, below, above, dim):
    length, width = centre.shape[dim], below.shape[dim]
    zero = jnp.zeros((), centre.dtype)
    low = [(0, 0, 0)] * centre.ndim
    low[dim] = (0, length - width, 0)
    high = [(0, 0, 0)] * centre.ndim
    high[dim] = (length - width, 0, 0)
    return centre + lax.pad(below, zero, low) + lax.pad(above, zero, high)


def band(weights, rows, cols, shift):
    taps = weights.shape[-1]
    gap = (
        jnp.arange(cols, dtype=jnp.int32)[None, :]
        - jnp.arange(rows, dtype=jnp.int32)[:, None]
        + shift
    )
    picks = (gap[:, :, None] == jnp.arange(taps, dtype=jnp.int32)).astype(jnp.float32)
    return jnp.einsum("oit,gt->goi", picks, weights, precision=lax.Precision.HIGHEST)


def block_sums(weights, axis, cells):
    blocks = lax.axis_size(axis)
    taps = weights.shape[-1]
    place = lax.axis_index(axis) * cells + jnp.arange(cells, dtype=jnp.int32)
    source = place[:, None] - jnp.arange(taps, dtype=jnp.int32)[None, :] + (taps - 1) // 2
    first = jnp.arange(blocks, dtype=jnp.int32)[:, None, None] * cells
    picks = ((source[None] >= first) & (source[None] < first + cells)).astype(jnp.float32)
    return jnp.einsum("bot,gt->ogb", picks, weights, precision=lax.Precision.HIGHEST)


def weight_of(kern, low, span, cells_x, cells_y, depth):
    views = kern.shape[0]
    taps = kern.shape[-1]
    sums_x = block_sums(kern[:, 0], "fx", cells_x)
    sums_y = block_sums(kern[:, 1], "fy", cells_y)
    levels = jnp.arange(depth, dtype=jnp.int32)
    inside = (levels >= low[..., None]) & (levels < (low + span)[..., None])
    table_z = band(kern[:, 2], depth, depth, (taps - 1) // 2)
    sums_z = jnp.einsum(
        "gxyi,gio->gxyo", inside.astype(jnp.float32), table_z, precision=lax.Precision.HIGHEST
    )
    plane = sums_x[:, None, :, :, None] * sums_y[None, :, :, None, :]
    plane = plane.reshape(cells_x, cells_y, -1)
    return jnp.einsum(
        "xym,mz->xyz", plane, sums_z.reshape(-1, depth), precision=lax.Precision.HIGHEST
    )


def body(estimate, images, psf, cover_lo, cover_len):
    group, cells_x, cells_y, depth = images.shape
    taps = psf.shape[-1]
    radius = (taps - 1) // 2
    halo = min(-(-radius // 16) * 16, cells_x, cells_y)
    exact = lax.Precision.HIGH
    groups = lax.axis_size("view")
    swap = [(i, (i + 1) % groups) for i in range(groups)]

    kern = psf / jnp.sum(psf, axis=-1, keepdims=True)
    start = gather_halo(estimate.astype(jnp.bfloat16), "fy", 1, halo)
    start, psf, cover_lo, cover_len = lax.optimization_barrier((start, psf, cover_lo, cover_len))
    pack = jnp.concatenate(
        [kern.reshape(-1), cover_lo.reshape(-1).astype(jnp.float32), cover_len.reshape(-1).astype(jnp.float32)]
    )
    packs = [pack]
    for _ in range(groups - 1):
        packs.append(lax.ppermute(packs[-1], "view", swap))
    packs = jnp.stack(packs)
    all_kern = packs[:, : kern.size].reshape((-1,) + kern.shape[1:])
    cells = cover_lo.size
    all_low = packs[:, kern.size : kern.size + cells].astype(jnp.int32).reshape((-1,) + cover_lo.shape[1:])
    all_span = packs[:, kern.size + cells :].astype(jnp.int32).reshape((-1,) + cover_len.shape[1:])
    lower_part = weight_of(all_kern, all_low, all_span, cells_x, cells_y, depth) + 0.5

    block_x, block_y = lax.axis_index("fx"), lax.axis_index("fy")
    low = lax.dynamic_slice(cover_lo, (0, block_x, block_y), (group, 1, 1))[..., None]
    span = lax.dynamic_slice(cover_len, (0, block_x, block_y), (group, 1, 1))[..., None]
    levels = jnp.arange(depth, dtype=jnp.int32)
    own = (levels >= low) & (levels < low + span)
    masked = jnp.where(own, images, jnp.zeros_like(images)).astype(jnp.float32)

    table_x = band(kern[:, 0], cells_x, cells_x + 2 * halo, radius - halo)
    table_centre = table_x[:, :, halo : halo + cells_x]
    table_edges = jnp.concatenate([table_x[:, :, :halo], table_x[:, :, halo + cells_x :]], axis=2)
    table_y = band(kern[:, 1], cells_y, cells_y + 2 * halo, radius - halo)
    table_z = band(kern[:, 2], depth, depth, radius)

    joined = estimate
    for step in range(ITERS):
        wide = start if step == 0 else gather_halo(joined.astype(jnp.bfloat16), "fy", 1, halo)
        wide = gather_halo(wide, "fx", 0, halo).astype(jnp.float32)
        field = jnp.einsum("gox,xyz->goyz", table_x, wide, precision=exact)
        field = jnp.einsum("goy,gxyz->gxoz", table_y, field, precision=exact)
        blurred = jnp.einsum("goz,gxyz->gxyo", table_z, field, precision=exact)
        ratio = masked / blurred
        field = jnp.einsum("goz,gxyo->gxyz", table_z, ratio, precision=exact)
        field = jnp.einsum("goy,gxoz->gxyz", table_y, field, precision=exact)
        edges = jnp.einsum("gox,goyz->xyz", table_edges, field, precision=exact)
        below, above = swap_edges(edges[:halo], edges[halo:], "fx")
        centre = jnp.einsum("gox,goyz->xyz", table_centre, field, precision=exact)
        field = add_edges(centre, below, above, 0)
        below, above = swap_edges(field[:, :halo], field[:, cells_y + halo :], "fy")
        field = add_edges(field[:, halo : cells_y + halo], below, above, 1)
        correction = field
        moving = field
        for _ in range(groups - 1):
            moving = lax.ppermute(moving, "view", swap)
            correction = correction + moving
        joined = joined * (correction + 0.5) / lower_part
    return joined


def solution(mesh):
    return jax.shard_map(
        body,
        mesh=mesh,
        in_specs=(
            P("fx", "fy", None),
            P("view", "fx", "fy", None),
            P("view", None, None),
            P("view", None, None),
            P("view", None, None),
        ),
        out_specs=P("fx", "fy", None),
        check_vma=False,
    )
```

```python
import functools

import jax
import jax.numpy as jnp
from jax import lax
from jax.experimental import pallas as pl
from jax.experimental.pallas import tpu as pltpu
from jax.sharding import PartitionSpec as P

ITERS = 2
LANES = 128
VMEM = pl.BlockSpec(memory_space=pltpu.VMEM)
SMEM = pl.BlockSpec(memory_space=pltpu.SMEM)
PARAMS = pltpu.CompilerParams(vmem_limit_bytes=40 * 2**20)
ROUNDS = ((None, 0), (None, 1), (0, 0), (0, 1), (1, 0), (1, 1), (0, None), (1, None))


def side(flags, axis, turn):
    return 1 - lax.rem(flags[axis] + turn, 2)


def span(flags, axis, turn, low, high, width):
    start = low + side(flags, axis, turn) * (high - low)
    return pl.ds(pl.multiple_of(start, 16), width)


def piece(flags, turns, full, lows, highs, halo):
    out = []
    for axis in range(2):
        if turns[axis] is None:
            out.append(full[axis])
        else:
            out.append(span(flags, axis, turns[axis], lows[axis], highs[axis], halo))
    return tuple(out)


def pairs_of(peers, turn):
    out = list(range(peers))
    for i in range(turn, peers - 1, 2):
        out[i], out[i + 1] = i + 1, i
    return out


def exchange(parts):
    size_x, size_y = lax.axis_size("fx"), lax.axis_size("fy")
    out = []
    for (turn_x, turn_y), part in zip(ROUNDS, parts):
        partner_x = list(range(size_x)) if turn_x is None else pairs_of(size_x, turn_x)
        partner_y = list(range(size_y)) if turn_y is None else pairs_of(size_y, turn_y)
        pairs = []
        for i in range(size_x):
            for j in range(size_y):
                if (turn_x is not None and partner_x[i] == i) or (turn_y is not None and partner_y[j] == j):
                    continue
                pairs.append((i * size_y + j, partner_x[i] * size_y + partner_y[j]))
        out.append(lax.ppermute(part, ("fx", "fy"), pairs))
    return out


def part_shapes(cells_x, cells_y, depth, halo, dtype):
    return [
        jax.ShapeDtypeStruct(
            (cells_x if tx is None else halo, cells_y if ty is None else halo, depth), dtype
        )
        for tx, ty in ROUNDS
    ]


def split(value):
    high = value.astype(jnp.bfloat16)
    low = (value - high.astype(jnp.float32)).astype(jnp.bfloat16)
    return high, low


def place(blocks, width):
    per = LANES // width
    tiles = []
    for first in range(0, len(blocks), per):
        tile = blocks[first]
        for at, block in enumerate(blocks[first + 1 : first + per]):
            tile = tile + pltpu.roll(block, (at + 1) * width, 1)
        tiles.append(tile)
    whole = tiles[0] if len(tiles) == 1 else jnp.concatenate(tiles, axis=1)
    return whole[:, : len(blocks) * width].astype(jnp.bfloat16)


def table_kernel(taps, halo, cells_x, cells_y, psf, tyf, txf, tzf, tzb, txb, tyb):
    group = psf.shape[0]
    radius = (taps - 1) // 2
    depth = tzb.shape[2]

    def parts(value):
        high = value.astype(jnp.bfloat16).astype(jnp.float32)
        return high, value - high

    y_blocks, y_low = [], []
    for k in range(group):
        rows = psf[k]
        rows = rows / jnp.sum(rows, axis=1, keepdims=True)
        bands = []
        for axis, cells in ((0, cells_x), (1, cells_y)):
            base = jnp.broadcast_to(pltpu.roll(rows[axis : axis + 1], halo - radius, 1), (cells, LANES))
            bands.append(pltpu.roll(base, 0, 1, stride=1, stride_axis=0))
        base = jnp.broadcast_to(pltpu.roll(rows[2:3], depth - radius, 1), (depth, depth))
        band_z = pltpu.roll(base, 0, 1, stride=1, stride_axis=0)
        gap = lax.broadcasted_iota(jnp.int32, (depth, depth), 1) - lax.broadcasted_iota(
            jnp.int32, (depth, depth), 0
        )
        band_z = jnp.where((gap >= -radius) & (gap <= radius), band_z, 0.0)
        wide_x, wide_y = cells_x + 2 * halo, cells_y + 2 * halo

        high, low = parts(bands[1])
        tyf[k * cells_y : (k + 1) * cells_y, :] = place([high, low], wide_y)
        high, low = parts(bands[0])
        txf[k] = place([high, low, high], wide_x)
        high, low = parts(band_z)
        tzb[k, 0:depth, :] = high.astype(jnp.bfloat16)
        tzb[k, depth : 2 * depth, :] = low.astype(jnp.bfloat16)
        tzb[k, 2 * depth :, :] = high.astype(jnp.bfloat16)
        high, low = high.T, low.T
        tzf[k, 0:depth, :] = high.astype(jnp.bfloat16)
        tzf[k, depth : 2 * depth, :] = low.astype(jnp.bfloat16)
        tzf[k, 2 * depth :, :] = high.astype(jnp.bfloat16)

        def turned(value, cells, wide):
            square = jnp.concatenate([value, jnp.zeros((LANES - cells, LANES), jnp.float32)], axis=0)
            return square.T[:wide]

        high, low = parts(turned(bands[0], cells_x, wide_x))
        txb[k] = place([high, low, high], cells_x)
        high, low = parts(turned(bands[1], cells_y, wide_y))
        y_blocks.append(high)
        y_low.append(low)
    tyb[...] = place(y_blocks + y_low + y_blocks, cells_y)


def blur_kernel(halo, chunk, flags, centre, *refs):
    received, refs = refs[:8], refs[8:]
    images, tyf, txf, tzf, tzb, txb, tyb = refs[:7]
    out_centre, sent = refs[7], refs[8:16]
    field, turned, back, result = refs[16:]
    cells_x, cells_y, depth = centre.shape
    group = images.shape[0]
    wide_x, wide_y = cells_x + 2 * halo, cells_y + 2 * halo
    inner = (pl.ds(halo, cells_x), pl.ds(halo, cells_y))
    zeros, tops = (0, 0), (cells_x + halo, cells_y + halo)

    field[inner] = centre[...]
    for turns, part in zip(ROUNDS, received):
        field[piece(flags, turns, inner, zeros, tops, halo)] = part[...]

    dot = functools.partial(jnp.dot, preferred_element_type=jnp.float32)
    pair = functools.partial(jnp.concatenate, axis=1)
    stack = functools.partial(jnp.concatenate, axis=0)

    def forward_y(i, carry):
        x = 2 * i
        both = pair([field[x], field[x + 1]])
        got = dot(tyf[...], stack([both, both]))
        turned[pl.ds(x, group * cells_y, stride=wide_x), :] = got[:, :depth]
        turned[pl.ds(x + 1, group * cells_y, stride=wide_x), :] = got[:, depth:]
        return carry

    lax.fori_loop(0, wide_x // 2, forward_y, 0, unroll=4)

    per = cells_y // chunk

    def middle(i, carry):
        k = i // per
        first = (i - k * per) * chunk
        rows = []
        for j in range(0, chunk, 2):
            at = pl.multiple_of((k * cells_y + first + j) * wide_x, 16)
            both = pair([turned[pl.ds(at, wide_x), :], turned[pl.ds(at + wide_x, wide_x), :]])
            high, low = split(both)
            got = dot(txf[k], stack([high, high, low]))
            rows += [got[:, :depth], got[:, depth:]]
        high, low = split(stack(rows))
        blurred = dot(pair([high, high, low]), tzf[k])
        seen = images[k, pl.ds(first, chunk)].astype(jnp.float32).reshape(chunk * cells_x, depth)
        high, low = split(seen / blurred)
        spread = dot(pair([high, high, low]), tzb[k])
        for j in range(0, chunk, 2):
            both = pair([spread[j * cells_x : (j + 1) * cells_x], spread[(j + 1) * cells_x : (j + 2) * cells_x]])
            high, low = split(both)
            got = dot(txb[k], stack([high, high, low]))
            at = k * cells_y + first + j
            back[pl.ds(at, wide_x, stride=group * cells_y), :] = got[:, :depth]
            back[pl.ds(at + 1, wide_x, stride=group * cells_y), :] = got[:, depth:]
        return carry

    lax.fori_loop(0, group * per, middle, 0, unroll=1)

    def backward_y(i, carry):
        rows = group * cells_y
        at = pl.multiple_of(2 * i * rows, 16)
        high, low = split(pair([back[pl.ds(at, rows), :], back[pl.ds(at + rows, rows), :]]))
        got = dot(tyb[...], stack([high, high, low]))
        result[2 * i] = got[:, :depth]
        result[2 * i + 1] = got[:, depth:]
        return carry

    lax.fori_loop(0, wide_x // 2, backward_y, 0, unroll=4)
    out_centre[...] = result[inner]
    for turns, part in zip(ROUNDS, sent):
        part[...] = result[piece(flags, turns, inner, zeros, tops, halo)]


def join_kernel(halo, flags, centre, *refs):
    received, out = refs[:8], refs[8]
    cells_x, cells_y, _ = centre.shape
    full = (pl.ds(0, cells_x), pl.ds(0, cells_y))
    out[...] = centre[...]
    for turns, part in zip(ROUNDS, received):
        at = piece(flags, turns, full, (0, 0), (cells_x - halo, cells_y - halo), halo)
        out[at] = out[at] + part[...]


def send_parts(flags, source, halo, out_centre, outs):
    cells_x, cells_y, _ = source.shape
    full = (pl.ds(0, cells_x), pl.ds(0, cells_y))
    out_centre[...] = source[...].astype(out_centre.dtype)
    for turns, part in zip(ROUNDS, outs):
        at = piece(flags, turns, full, (0, 0), (cells_x - halo, cells_y - halo), halo)
        part[...] = source[at].astype(part.dtype)


def start_kernel(halo, flags, source, out_centre, *outs):
    send_parts(flags, source, halo, out_centre, outs)


def update_kernel(halo, flags, joined, own, moved, lower, out, *outs):
    out[...] = joined[...] * (own[...] + moved[...] + 0.5) / lower[...]
    if outs:
        send_parts(flags, out, halo, outs[0], outs[1:])


def call(kernel, inputs, outs, scratch=(), flagged=True):
    return pl.pallas_call(
        kernel,
        out_shape=outs,
        in_specs=[SMEM if flagged and i == 0 else VMEM for i in range(len(inputs))],
        out_specs=[VMEM] * len(outs),
        scratch_shapes=list(scratch),
        compiler_params=PARAMS,
    )(*inputs)


def band(weights, rows, cols, shift):
    taps = weights.shape[-1]
    gap = (
        jnp.arange(cols, dtype=jnp.int32)[None, :]
        - jnp.arange(rows, dtype=jnp.int32)[:, None]
        + shift
    )
    picks = (gap[:, :, None] == jnp.arange(taps, dtype=jnp.int32)).astype(jnp.float32)
    return jnp.einsum("oit,gt->goi", picks, weights, precision=lax.Precision.HIGHEST)


def block_sums(weights, axis, cells):
    blocks = lax.axis_size(axis)
    taps = weights.shape[-1]
    at = lax.axis_index(axis) * cells + jnp.arange(cells, dtype=jnp.int32)
    source = at[:, None] - jnp.arange(taps, dtype=jnp.int32)[None, :] + (taps - 1) // 2
    first = jnp.arange(blocks, dtype=jnp.int32)[:, None, None] * cells
    picks = ((source[None] >= first) & (source[None] < first + cells)).astype(jnp.float32)
    return jnp.einsum("bot,gt->ogb", picks, weights, precision=lax.Precision.HIGHEST)


def weight_of(kern, low, length, cells_x, cells_y, depth):
    taps = kern.shape[-1]
    sums_x = block_sums(kern[:, 0], "fx", cells_x)
    sums_y = block_sums(kern[:, 1], "fy", cells_y)
    levels = jnp.arange(depth, dtype=jnp.int32)
    inside = (levels >= low[..., None]) & (levels < (low + length)[..., None])
    table_z = band(kern[:, 2], depth, depth, (taps - 1) // 2)
    sums_z = jnp.einsum(
        "gxyi,gio->gxyo", inside.astype(jnp.float32), table_z, precision=lax.Precision.HIGHEST
    )
    plane = sums_x[:, None, :, :, None] * sums_y[None, :, :, None, :]
    plane = plane.reshape(cells_x, cells_y, -1)
    return jnp.einsum(
        "xym,mz->xyz", plane, sums_z.reshape(-1, depth), precision=lax.Precision.HIGHEST
    )


def body(estimate, images, psf, cover_lo, cover_len):
    group, cells_x, cells_y, depth = images.shape
    taps = psf.shape[-1]
    halo = -(-((taps - 1) // 2) // 16) * 16
    wide_x, wide_y = cells_x + 2 * halo, cells_y + 2 * halo
    groups = lax.axis_size("view")
    swap = [(i, (i + 1) % groups) for i in range(groups)]
    bf16, f32 = jnp.bfloat16, jnp.float32
    block = lambda dtype: jax.ShapeDtypeStruct((cells_x, cells_y, depth), dtype)
    parts_of = functools.partial(part_shapes, cells_x, cells_y, depth, halo)

    block_x, block_y = lax.axis_index("fx"), lax.axis_index("fy")
    flags = jnp.stack([block_x % 2, block_y % 2]).astype(jnp.int32)

    centre, *parts = call(
        functools.partial(start_kernel, halo), (flags, estimate), [block(bf16)] + parts_of(bf16)
    )
    parts = exchange(parts)

    padded = jnp.pad(psf, ((0, 0), (0, 0), (0, LANES - taps)))
    tables = call(
        functools.partial(table_kernel, taps, halo, cells_x, cells_y),
        (padded,),
        [
            jax.ShapeDtypeStruct((group * cells_y, 2 * wide_y), bf16),
            jax.ShapeDtypeStruct((group, cells_x, 3 * wide_x), bf16),
            jax.ShapeDtypeStruct((group, 3 * depth, depth), bf16),
            jax.ShapeDtypeStruct((group, 3 * depth, depth), bf16),
            jax.ShapeDtypeStruct((group, wide_x, 3 * cells_x), bf16),
            jax.ShapeDtypeStruct((wide_y, 3 * group * cells_y), bf16),
        ],
        flagged=False,
    )

    low = lax.dynamic_slice(cover_lo, (0, block_x, block_y), (group, 1, 1))[..., None]
    length = lax.dynamic_slice(cover_len, (0, block_x, block_y), (group, 1, 1))[..., None]
    levels = jnp.arange(depth, dtype=jnp.int32)
    own = (levels >= low) & (levels < low + length)
    masked = jnp.where(own, images, jnp.zeros_like(images)).transpose(0, 2, 1, 3)

    psf_late, lo_late, len_late, _ = lax.optimization_barrier((psf, cover_lo, cover_len, parts[0]))
    kern = psf_late / jnp.sum(psf_late, axis=-1, keepdims=True)
    pack = jnp.concatenate(
        [kern.reshape(-1), lo_late.reshape(-1).astype(f32), len_late.reshape(-1).astype(f32)]
    )
    packs = [pack]
    for _ in range(groups - 1):
        packs.append(lax.ppermute(packs[-1], "view", swap))
    packs = jnp.stack(packs)
    cells = cover_lo.size
    all_kern = packs[:, : kern.size].reshape((-1,) + kern.shape[1:])
    all_low = packs[:, kern.size : kern.size + cells].astype(jnp.int32).reshape((-1,) + cover_lo.shape[1:])
    all_len = packs[:, kern.size + cells :].astype(jnp.int32).reshape((-1,) + cover_len.shape[1:])
    lower_part = weight_of(all_kern, all_low, all_len, cells_x, cells_y, depth) + 0.5

    joined = estimate
    for step in range(ITERS):
        total, *sums = call(
            functools.partial(blur_kernel, halo, 8),
            (flags, centre, *parts, masked, *tables),
            [block(f32)] + parts_of(f32),
            [
                pltpu.VMEM((wide_x, wide_y, depth), bf16),
                pltpu.VMEM((group * cells_y * wide_x, depth), f32),
                pltpu.VMEM((wide_x * group * cells_y, depth), f32),
                pltpu.VMEM((wide_x, wide_y, depth), f32),
            ],
        )
        sums = exchange(sums)
        (own_sum,) = call(functools.partial(join_kernel, halo), (flags, total, *sums), [block(f32)])
        moving, moved = own_sum, None
        for _ in range(groups - 1):
            moving = lax.ppermute(moving, "view", swap)
            moved = moving if moved is None else moved + moving
        if moved is None:
            moved = jnp.zeros_like(own_sum)
        last = step == ITERS - 1
        joined, *rest = call(
            functools.partial(update_kernel, halo),
            (flags, joined, own_sum, moved, lower_part),
            [block(f32)] + ([] if last else [block(bf16)] + parts_of(bf16)),
        )
        if not last:
            centre, parts = rest[0], exchange(rest[1:])
    return joined


def solution(mesh):
    return jax.shard_map(
        body,
        mesh=mesh,
        in_specs=(
            P("fx", "fy", None),
            P("view", "fx", "fy", None),
            P("view", None, None),
            P("view", None, None),
            P("view", None, None),
        ),
        out_specs=P("fx", "fy", None),
        check_vma=False,
    )
```

```python
import jax
import jax.numpy as jnp
from jax import lax
from jax.sharding import PartitionSpec as P

ITERS = 2


def swap_edges(to_below, to_above, axis):
    peers = lax.axis_size(axis)
    even = lax.axis_index(axis) % 2 == 0

    def pairs(start):
        out = []
        for i in range(start, peers - 1, 2):
            out += [(i, i + 1), (i + 1, i)]
        return out

    first = lax.ppermute(jnp.where(even, to_above, to_below), axis, pairs(0))
    second = lax.ppermute(jnp.where(even, to_below, to_above), axis, pairs(1))
    return jnp.where(even, second, first), jnp.where(even, first, second)


def gather_halo(array, axis, dim, width):
    length = array.shape[dim]
    before, after = swap_edges(
        lax.slice_in_dim(array, 0, width, axis=dim),
        lax.slice_in_dim(array, length - width, length, axis=dim),
        axis,
    )
    return jnp.concatenate([before, array, after], axis=dim)


def add_edges(centre, below, above, dim):
    length, width = centre.shape[dim], below.shape[dim]
    zero = jnp.zeros((), centre.dtype)
    low = [(0, 0, 0)] * centre.ndim
    low[dim] = (0, length - width, 0)
    high = [(0, 0, 0)] * centre.ndim
    high[dim] = (length - width, 0, 0)
    return centre + lax.pad(below, zero, low) + lax.pad(above, zero, high)


def pack_fixed(values, bound):
    level = jnp.ceil(4.0 * jnp.log2(jnp.maximum(bound, 1e-30)) + 0.01)
    scale = 32700.0 * jnp.exp2(-0.25 * level)
    fixed = jnp.round(values * scale).astype(jnp.int16)
    plane = jnp.broadcast_to(level.astype(jnp.int16), (1,) + values.shape[1:])
    return jnp.concatenate([fixed, plane], axis=0)


def unpack_fixed(packed):
    level = packed[-1, 0, 0].astype(jnp.float32)
    step = jnp.exp2(0.25 * level) * (1.0 / 32700.0)
    return packed[:-1].astype(jnp.float32) * step


def bound_of(packed):
    return jnp.exp2(0.25 * packed[-1, 0, 0].astype(jnp.float32))


def swap_fixed(to_below, to_above, bound, axis):
    below, above = swap_edges(pack_fixed(to_below, bound), pack_fixed(to_above, bound), axis)
    limit = bound + bound_of(below) + bound_of(above)
    return unpack_fixed(below), unpack_fixed(above), limit


def band(weights, rows, cols, shift):
    taps = weights.shape[-1]
    gap = (
        jnp.arange(cols, dtype=jnp.int32)[None, :]
        - jnp.arange(rows, dtype=jnp.int32)[:, None]
        + shift
    )
    picks = (gap[:, :, None] == jnp.arange(taps, dtype=jnp.int32)).astype(jnp.float32)
    return jnp.einsum("oit,gt->goi", picks, weights, precision=lax.Precision.HIGHEST)


def block_sums(weights, axis, cells):
    blocks = lax.axis_size(axis)
    taps = weights.shape[-1]
    place = lax.axis_index(axis) * cells + jnp.arange(cells, dtype=jnp.int32)
    source = place[:, None] - jnp.arange(taps, dtype=jnp.int32)[None, :] + (taps - 1) // 2
    first = jnp.arange(blocks, dtype=jnp.int32)[:, None, None] * cells
    picks = ((source[None] >= first) & (source[None] < first + cells)).astype(jnp.float32)
    return jnp.einsum("bot,gt->ogb", picks, weights, precision=lax.Precision.HIGHEST)


def weight_of(kern, low, span, cells_x, cells_y, depth):
    views = kern.shape[0]
    taps = kern.shape[-1]
    sums_x = block_sums(kern[:, 0], "fx", cells_x)
    sums_y = block_sums(kern[:, 1], "fy", cells_y)
    levels = jnp.arange(depth, dtype=jnp.int32)
    inside = (levels >= low[..., None]) & (levels < (low + span)[..., None])
    table_z = band(kern[:, 2], depth, depth, (taps - 1) // 2)
    sums_z = jnp.einsum(
        "gxyi,gio->gxyo", inside.astype(jnp.float32), table_z, precision=lax.Precision.HIGHEST
    )
    plane = sums_x[:, None, :, :, None] * sums_y[None, :, :, None, :]
    plane = plane.reshape(cells_x, cells_y, -1)
    return jnp.einsum(
        "xym,mz->xyz", plane, sums_z.reshape(-1, depth), precision=lax.Precision.HIGHEST
    )


def body(estimate, images, psf, cover_lo, cover_len):
    group, cells_x, cells_y, depth = images.shape
    taps = psf.shape[-1]
    radius = (taps - 1) // 2
    halo = min(-(-radius // 16) * 16, cells_x, cells_y)
    exact = lax.Precision.HIGH
    groups = lax.axis_size("view")
    swap = [(i, (i + 1) % groups) for i in range(groups)]

    kern = psf / jnp.sum(psf, axis=-1, keepdims=True)
    start = gather_halo(estimate.astype(jnp.bfloat16), "fy", 1, halo)
    start, psf, cover_lo, cover_len = lax.optimization_barrier((start, psf, cover_lo, cover_len))
    pack = jnp.concatenate(
        [kern.reshape(-1), cover_lo.reshape(-1).astype(jnp.float32), cover_len.reshape(-1).astype(jnp.float32)]
    )
    packs = [pack]
    for _ in range(groups - 1):
        packs.append(lax.ppermute(packs[-1], "view", swap))
    packs = jnp.stack(packs)
    all_kern = packs[:, : kern.size].reshape((-1,) + kern.shape[1:])
    cells = cover_lo.size
    all_low = packs[:, kern.size : kern.size + cells].astype(jnp.int32).reshape((-1,) + cover_lo.shape[1:])
    all_span = packs[:, kern.size + cells :].astype(jnp.int32).reshape((-1,) + cover_len.shape[1:])
    lower_part = weight_of(all_kern, all_low, all_span, cells_x, cells_y, depth) + 0.5

    block_x, block_y = lax.axis_index("fx"), lax.axis_index("fy")
    low = lax.dynamic_slice(cover_lo, (0, block_x, block_y), (group, 1, 1))[..., None]
    span = lax.dynamic_slice(cover_len, (0, block_x, block_y), (group, 1, 1))[..., None]
    levels = jnp.arange(depth, dtype=jnp.int32)
    own = (levels >= low) & (levels < low + span)
    masked = jnp.where(own, images, jnp.zeros_like(images)).astype(jnp.float32)

    table_x = band(kern[:, 0], cells_x, cells_x + 2 * halo, radius - halo)
    table_y = band(kern[:, 1], cells_y, cells_y + 2 * halo, radius - halo)
    table_z = band(kern[:, 2], depth, depth, radius)

    joined = estimate
    for step in range(ITERS):
        wide = start if step == 0 else gather_halo(joined.astype(jnp.bfloat16), "fy", 1, halo)
        wide = gather_halo(wide, "fx", 0, halo).astype(jnp.float32)
        field = jnp.einsum("gox,xyz->goyz", table_x, wide, precision=exact)
        field = jnp.einsum("goy,gxyz->gxoz", table_y, field, precision=exact)
        blurred = jnp.einsum("goz,gxyz->gxyo", table_z, field, precision=exact)
        ratio = masked / blurred
        field = jnp.einsum("goz,gxyo->gxyz", table_z, ratio, precision=exact)
        field = jnp.einsum("goy,gxoz->gxyz", table_y, field, precision=exact)
        field = jnp.einsum("gox,goyz->xyz", table_x, field, precision=exact)
        below, above, limit = swap_fixed(field[:halo], field[cells_x + halo :], jnp.max(field), "fx")
        field = add_edges(field[halo : cells_x + halo], below, above, 0)
        below, above, _ = swap_fixed(field[:, :halo], field[:, cells_y + halo :], limit, "fy")
        field = add_edges(field[:, halo : cells_y + halo], below, above, 1)
        moving = pack_fixed(field, jnp.max(field))
        correction = unpack_fixed(moving)
        for _ in range(groups - 1):
            moving = lax.ppermute(moving, "view", swap)
            correction = correction + unpack_fixed(moving)
        joined = joined * (correction + 0.5) / lower_part
    return joined


def solution(mesh):
    return jax.shard_map(
        body,
        mesh=mesh,
        in_specs=(
            P("fx", "fy", None),
            P("view", "fx", "fy", None),
            P("view", None, None),
            P("view", None, None),
            P("view", None, None),
        ),
        out_specs=P("fx", "fy", None),
        check_vma=False,
    )
```

```python
import functools

import jax
import jax.numpy as jnp
from jax import lax
from jax.experimental import pallas as pl
from jax.experimental.pallas import tpu as pltpu
from jax.sharding import PartitionSpec as P

ITERS = 2
LANES = 128
VMEM = pl.BlockSpec(memory_space=pltpu.VMEM)
SMEM = pl.BlockSpec(memory_space=pltpu.SMEM)
PARAMS = pltpu.CompilerParams(vmem_limit_bytes=40 * 2**20)


def swap_edges(to_below, to_above, axis):
    peers = lax.axis_size(axis)
    even = lax.axis_index(axis) % 2 == 0

    def pairs(start):
        out = []
        for i in range(start, peers - 1, 2):
            out += [(i, i + 1), (i + 1, i)]
        return out

    first = lax.ppermute(jnp.where(even, to_above, to_below), axis, pairs(0))
    second = lax.ppermute(jnp.where(even, to_below, to_above), axis, pairs(1))
    return jnp.where(even, second, first), jnp.where(even, first, second)


def gather_halo(array, axis, dim, width):
    length = array.shape[dim]
    before, after = swap_edges(
        lax.slice_in_dim(array, 0, width, axis=dim),
        lax.slice_in_dim(array, length - width, length, axis=dim),
        axis,
    )
    return jnp.concatenate([before, array, after], axis=dim)


def add_edges(centre, below, above, dim):
    length, width = centre.shape[dim], below.shape[dim]
    zero = jnp.zeros((), centre.dtype)
    low = [(0, 0, 0)] * centre.ndim
    low[dim] = (0, length - width, 0)
    high = [(0, 0, 0)] * centre.ndim
    high[dim] = (length - width, 0, 0)
    return centre + lax.pad(below, zero, low) + lax.pad(above, zero, high)


def split(value):
    high = value.astype(jnp.bfloat16)
    low = (value - high.astype(jnp.float32)).astype(jnp.bfloat16)
    return high, low


def place(blocks, width):
    per = LANES // width
    tiles = []
    for first in range(0, len(blocks), per):
        tile = blocks[first]
        for at, block in enumerate(blocks[first + 1 : first + per]):
            tile = tile + pltpu.roll(block, (at + 1) * width, 1)
        tiles.append(tile)
    whole = tiles[0] if len(tiles) == 1 else jnp.concatenate(tiles, axis=1)
    return whole[:, : len(blocks) * width].astype(jnp.bfloat16)


def table_kernel(taps, halo, cells_x, cells_y, psf, tx, txs, tyf, tzf, tzb, tyb):
    group = psf.shape[0]
    radius = (taps - 1) // 2
    depth = tzb.shape[2]
    wide_x, wide_y = cells_x + 2 * halo, cells_y + 2 * halo

    def parts(value):
        high = value.astype(jnp.bfloat16).astype(jnp.float32)
        return high, value - high

    for k in range(group):
        rows = psf[k]
        rows = rows / jnp.sum(rows, axis=1, keepdims=True)
        bands = []
        for axis, cells in ((0, cells_x), (1, cells_y)):
            base = jnp.broadcast_to(pltpu.roll(rows[axis : axis + 1], halo - radius, 1), (cells, LANES))
            bands.append(pltpu.roll(base, 0, 1, stride=1, stride_axis=0))
        base = jnp.broadcast_to(pltpu.roll(rows[2:3], depth - radius, 1), (depth, depth))
        band_z = pltpu.roll(base, 0, 1, stride=1, stride_axis=0)
        gap = lax.broadcasted_iota(jnp.int32, (depth, depth), 1) - lax.broadcasted_iota(
            jnp.int32, (depth, depth), 0
        )
        band_z = jnp.where((gap >= -radius) & (gap <= radius), band_z, 0.0)

        tx[k] = bands[0][:, :wide_x]
        high, low = parts(bands[0])
        txs[0, k] = place([high, low], wide_x)
        txs[1, k] = place([high, jnp.zeros_like(low)], wide_x)
        high, low = parts(bands[1])
        tyf[k] = place([high, low, high], wide_y)
        high, low = parts(band_z)
        tzb[k, 0:depth, :] = high.astype(jnp.bfloat16)
        tzb[k, depth : 2 * depth, :] = low.astype(jnp.bfloat16)
        tzb[k, 2 * depth :, :] = high.astype(jnp.bfloat16)
        high, low = high.T, low.T
        tzf[k, 0:depth, :] = high.astype(jnp.bfloat16)
        tzf[k, depth : 2 * depth, :] = low.astype(jnp.bfloat16)
        tzf[k, 2 * depth :, :] = high.astype(jnp.bfloat16)
        square = jnp.concatenate([bands[1], jnp.zeros((LANES - cells_y, LANES), jnp.float32)], axis=0)
        high, low = parts(square.T[:wide_y])
        tyb[k] = place([high, low, high], cells_y)


def middle_kernel(chunk, spot, lows, lengths, wide, images, tyf, tzf, tzb, tyb, out):
    k = pl.program_id(0)
    _, cells_x, cells_y, depth = images.shape
    wide_y = wide.shape[2]
    low = lows[k, spot[0], spot[1]]
    level = lax.broadcasted_iota(jnp.int32, (chunk * cells_y, depth), 1)
    inside = (level >= low) & (level < low + lengths[k, spot[0], spot[1]])
    dot = functools.partial(jnp.dot, preferred_element_type=jnp.float32)
    pair = functools.partial(jnp.concatenate, axis=1)
    stack = functools.partial(jnp.concatenate, axis=0)

    def three(left, value):
        high, low = split(value)
        return dot(left, stack([high, high, low]))

    def along(value, right):
        high, low = split(value)
        return dot(pair([high, high, low]), right)

    for first in range(0, cells_x, chunk):
        rows = []
        for x in range(first, first + chunk, 2):
            got = three(tyf[k], pair([wide[0, x], wide[0, x + 1]]))
            rows += [got[:, :depth], got[:, depth:]]
        blurred = along(stack(rows), tzf[k])
        seen = images[0, first : first + chunk].astype(jnp.float32).reshape(chunk * cells_y, depth)
        spread = along(jnp.where(inside, seen, 0.0) / blurred, tzb[k])
        for at in range(0, chunk, 2):
            two = pair([spread[at * cells_y : (at + 1) * cells_y], spread[(at + 1) * cells_y : (at + 2) * cells_y]])
            high, low = split(three(tyb[k], two))
            for j in range(2):
                out[0, 0, first + at + j] = high[:, j * depth : (j + 1) * depth]
                out[1, 0, first + at + j] = low[:, j * depth : (j + 1) * depth]


def band(weights, rows, cols, shift):
    taps = weights.shape[-1]
    gap = (
        jnp.arange(cols, dtype=jnp.int32)[None, :]
        - jnp.arange(rows, dtype=jnp.int32)[:, None]
        + shift
    )
    picks = (gap[:, :, None] == jnp.arange(taps, dtype=jnp.int32)).astype(jnp.float32)
    return jnp.einsum("oit,gt->goi", picks, weights, precision=lax.Precision.HIGHEST)


def block_sums(weights, axis, cells):
    blocks = lax.axis_size(axis)
    taps = weights.shape[-1]
    place = lax.axis_index(axis) * cells + jnp.arange(cells, dtype=jnp.int32)
    source = place[:, None] - jnp.arange(taps, dtype=jnp.int32)[None, :] + (taps - 1) // 2
    first = jnp.arange(blocks, dtype=jnp.int32)[:, None, None] * cells
    picks = ((source[None] >= first) & (source[None] < first + cells)).astype(jnp.float32)
    return jnp.einsum("bot,gt->ogb", picks, weights, precision=lax.Precision.HIGHEST)


def weight_of(kern, low, span, cells_x, cells_y, depth):
    views = kern.shape[0]
    taps = kern.shape[-1]
    sums_x = block_sums(kern[:, 0], "fx", cells_x)
    sums_y = block_sums(kern[:, 1], "fy", cells_y)
    levels = jnp.arange(depth, dtype=jnp.int32)
    inside = (levels >= low[..., None]) & (levels < (low + span)[..., None])
    table_z = band(kern[:, 2], depth, depth, (taps - 1) // 2)
    sums_z = jnp.einsum(
        "gxyi,gio->gxyo", inside.astype(jnp.float32), table_z, precision=lax.Precision.HIGHEST
    )
    plane = sums_x[:, None, :, :, None] * sums_y[None, :, :, None, :]
    plane = plane.reshape(cells_x, cells_y, -1)
    return jnp.einsum(
        "xym,mz->xyz", plane, sums_z.reshape(-1, depth), precision=lax.Precision.HIGHEST
    )


def body(estimate, images, psf, cover_lo, cover_len):
    group, cells_x, cells_y, depth = images.shape
    taps = psf.shape[-1]
    halo = -(-((taps - 1) // 2) // 16) * 16
    wide_x, wide_y = cells_x + 2 * halo, cells_y + 2 * halo
    groups = lax.axis_size("view")
    swap = [(i, (i + 1) % groups) for i in range(groups)]
    bf16, f32 = jnp.bfloat16, jnp.float32
    shape = jax.ShapeDtypeStruct

    start = gather_halo(estimate.astype(bf16), "fy", 1, halo)
    psf_late, lo_late, len_late, _ = lax.optimization_barrier((psf, cover_lo, cover_len, start))
    kern = psf_late / jnp.sum(psf_late, axis=-1, keepdims=True)
    pack = jnp.concatenate(
        [kern.reshape(-1), lo_late.reshape(-1).astype(f32), len_late.reshape(-1).astype(f32)]
    )
    packs = [pack]
    for _ in range(groups - 1):
        packs.append(lax.ppermute(packs[-1], "view", swap))
    packs = jnp.stack(packs)
    cells = cover_lo.size
    all_kern = packs[:, : kern.size].reshape((-1,) + kern.shape[1:])
    all_low = packs[:, kern.size : kern.size + cells].astype(jnp.int32).reshape((-1,) + cover_lo.shape[1:])
    all_len = packs[:, kern.size + cells :].astype(jnp.int32).reshape((-1,) + cover_len.shape[1:])
    lower_part = weight_of(all_kern, all_low, all_len, cells_x, cells_y, depth) + 0.5

    spot = jnp.stack([lax.axis_index("fx"), lax.axis_index("fy")]).astype(jnp.int32)
    padded = jnp.pad(psf, ((0, 0), (0, 0), (0, LANES - taps)))
    table_x, table_sum, *tables = pl.pallas_call(
        functools.partial(table_kernel, taps, halo, cells_x, cells_y),
        out_shape=[
            shape((group, cells_x, wide_x), f32),
            shape((2, group, cells_x, 2 * wide_x), bf16),
            shape((group, cells_y, 3 * wide_y), bf16),
            shape((group, 3 * depth, depth), bf16),
            shape((group, 3 * depth, depth), bf16),
            shape((group, wide_y, 3 * cells_y), bf16),
        ],
        in_specs=[VMEM],
        out_specs=[VMEM] * 6,
        compiler_params=PARAMS,
    )(padded)
    middle = pl.pallas_call(
        functools.partial(middle_kernel, 8),
        grid=(group,),
        out_shape=shape((2, group, cells_x, wide_y, depth), bf16),
        in_specs=[SMEM, SMEM, SMEM]
        + [
            pl.BlockSpec((1, cells_x, wide_y, depth), lambda k: (k, 0, 0, 0)),
            pl.BlockSpec((1, cells_x, cells_y, depth), lambda k: (k, 0, 0, 0)),
        ]
        + [VMEM] * 4,
        out_specs=pl.BlockSpec((2, 1, cells_x, wide_y, depth), lambda k: (0, k, 0, 0, 0)),
        compiler_params=PARAMS,
    )

    joined = estimate
    for step in range(ITERS):
        wide = start if step == 0 else gather_halo(joined.astype(bf16), "fy", 1, halo)
        wide = gather_halo(wide, "fx", 0, halo).astype(f32)
        field = jnp.einsum("gox,xyz->goyz", table_x, wide, precision=lax.Precision.HIGH)
        field = middle(spot, cover_lo, cover_len, field, images, *tables)
        field = jnp.einsum("sgox,sgoyz->xyz", table_sum, field, preferred_element_type=f32)
        field = field[:wide_x] + field[wide_x:]
        below, above = swap_edges(field[:halo], field[cells_x + halo :], "fx")
        field = add_edges(field[halo : cells_x + halo], below, above, 0)
        below, above = swap_edges(field[:, :halo], field[:, cells_y + halo :], "fy")
        field = add_edges(field[:, halo : cells_y + halo], below, above, 1)
        correction = field
        moving = field
        for _ in range(groups - 1):
            moving = lax.ppermute(moving, "view", swap)
            correction = correction + moving
        joined = joined * (correction + 0.5) / lower_part
    return joined


def solution(mesh):
    return jax.shard_map(
        body,
        mesh=mesh,
        in_specs=(
            P("fx", "fy", None),
            P("view", "fx", "fy", None),
            P("view", None, None),
            P("view", None, None),
            P("view", None, None),
        ),
        out_specs=P("fx", "fy", None),
        check_vma=False,
    )
```

```python
import jax
import jax.numpy as jnp
from jax import lax
from jax.sharding import PartitionSpec as P

ITERS = 2


def swap_edges(to_below, to_above, axis):
    peers = lax.axis_size(axis)
    even = lax.axis_index(axis) % 2 == 0

    def pairs(start):
        out = []
        for i in range(start, peers - 1, 2):
            out += [(i, i + 1), (i + 1, i)]
        return out

    first = lax.ppermute(jnp.where(even, to_above, to_below), axis, pairs(0))
    second = lax.ppermute(jnp.where(even, to_below, to_above), axis, pairs(1))
    return jnp.where(even, second, first), jnp.where(even, first, second)


def gather_halo(array, axis, dim, width):
    length = array.shape[dim]
    before, after = swap_edges(
        lax.slice_in_dim(array, 0, width, axis=dim),
        lax.slice_in_dim(array, length - width, length, axis=dim),
        axis,
    )
    return jnp.concatenate([before, array, after], axis=dim)


def add_edges(centre, below, above, dim):
    length, width = centre.shape[dim], below.shape[dim]
    zero = jnp.zeros((), centre.dtype)
    low = [(0, 0, 0)] * centre.ndim
    low[dim] = (0, length - width, 0)
    high = [(0, 0, 0)] * centre.ndim
    high[dim] = (length - width, 0, 0)
    return centre + lax.pad(below, zero, low) + lax.pad(above, zero, high)


def pack_fixed(values):
    top = jnp.max(jnp.abs(values), axis=1, keepdims=True)
    level = jnp.ceil(4.0 * jnp.log2(jnp.maximum(top, 1e-30)) + 0.01)
    scale = 32700.0 * jnp.exp2(-0.25 * level)
    fixed = jnp.round(values * scale).astype(jnp.int16)
    return jnp.concatenate([fixed, level.astype(jnp.int16)], axis=1)


def unpack_fixed(packed):
    step = jnp.exp2(0.25 * packed[:, -1:].astype(jnp.float32)) * (1.0 / 32700.0)
    return packed[:, :-1].astype(jnp.float32) * step


def swap_fixed(to_below, to_above, axis):
    below, above = swap_edges(pack_fixed(to_below), pack_fixed(to_above), axis)
    return unpack_fixed(below), unpack_fixed(above)


def band(weights, rows, cols, shift):
    taps = weights.shape[-1]
    gap = (
        jnp.arange(cols, dtype=jnp.int32)[None, :]
        - jnp.arange(rows, dtype=jnp.int32)[:, None]
        + shift
    )
    picks = (gap[:, :, None] == jnp.arange(taps, dtype=jnp.int32)).astype(jnp.float32)
    return jnp.einsum("oit,gt->goi", picks, weights, precision=lax.Precision.HIGHEST)


def block_sums(weights, axis, cells):
    blocks = lax.axis_size(axis)
    taps = weights.shape[-1]
    place = lax.axis_index(axis) * cells + jnp.arange(cells, dtype=jnp.int32)
    source = place[:, None] - jnp.arange(taps, dtype=jnp.int32)[None, :] + (taps - 1) // 2
    first = jnp.arange(blocks, dtype=jnp.int32)[:, None, None] * cells
    picks = ((source[None] >= first) & (source[None] < first + cells)).astype(jnp.float32)
    return jnp.einsum("bot,gt->ogb", picks, weights, precision=lax.Precision.HIGHEST)


def weight_of(kern, low, span, cells_x, cells_y, depth):
    views = kern.shape[0]
    taps = kern.shape[-1]
    sums_x = block_sums(kern[:, 0], "fx", cells_x)
    sums_y = block_sums(kern[:, 1], "fy", cells_y)
    levels = jnp.arange(depth, dtype=jnp.int32)
    inside = (levels >= low[..., None]) & (levels < (low + span)[..., None])
    table_z = band(kern[:, 2], depth, depth, (taps - 1) // 2)
    sums_z = jnp.einsum(
        "gxyi,gio->gxyo", inside.astype(jnp.float32), table_z, precision=lax.Precision.HIGHEST
    )
    plane = sums_x[:, None, :, :, None] * sums_y[None, :, :, None, :]
    plane = plane.reshape(cells_x, cells_y, -1)
    return jnp.einsum(
        "xym,mz->xyz", plane, sums_z.reshape(-1, depth), precision=lax.Precision.HIGHEST
    )


def body(estimate, images, psf, cover_lo, cover_len):
    group, cells_x, cells_y, depth = images.shape
    taps = psf.shape[-1]
    radius = (taps - 1) // 2
    halo = min(-(-radius // 16) * 16, cells_x, cells_y)
    exact = lax.Precision.HIGH
    groups = lax.axis_size("view")
    swap = [(i, (i + 1) % groups) for i in range(groups)]

    kern = psf / jnp.sum(psf, axis=-1, keepdims=True)
    start = gather_halo(estimate.astype(jnp.bfloat16), "fy", 1, halo)
    start, psf, cover_lo, cover_len = lax.optimization_barrier((start, psf, cover_lo, cover_len))
    pack = jnp.concatenate(
        [kern.reshape(-1), cover_lo.reshape(-1).astype(jnp.float32), cover_len.reshape(-1).astype(jnp.float32)]
    )
    packs = [pack]
    for _ in range(groups - 1):
        packs.append(lax.ppermute(packs[-1], "view", swap))
    packs = jnp.stack(packs)
    all_kern = packs[:, : kern.size].reshape((-1,) + kern.shape[1:])
    cells = cover_lo.size
    all_low = packs[:, kern.size : kern.size + cells].astype(jnp.int32).reshape((-1,) + cover_lo.shape[1:])
    all_span = packs[:, kern.size + cells :].astype(jnp.int32).reshape((-1,) + cover_len.shape[1:])
    lower_part = weight_of(all_kern, all_low, all_span, cells_x, cells_y, depth) + 0.5

    block_x, block_y = lax.axis_index("fx"), lax.axis_index("fy")
    low = lax.dynamic_slice(cover_lo, (0, block_x, block_y), (group, 1, 1))[..., None]
    span = lax.dynamic_slice(cover_len, (0, block_x, block_y), (group, 1, 1))[..., None]
    levels = jnp.arange(depth, dtype=jnp.int32)
    own = (levels >= low) & (levels < low + span)
    masked = jnp.where(own, images, jnp.zeros_like(images)).astype(jnp.float32)

    table_x = band(kern[:, 0], cells_x, cells_x + 2 * halo, radius - halo)
    table_y = band(kern[:, 1], cells_y, cells_y + 2 * halo, radius - halo)
    table_z = band(kern[:, 2], depth, depth, radius)

    joined = estimate
    for step in range(ITERS):
        wide = start if step == 0 else gather_halo(joined.astype(jnp.bfloat16), "fy", 1, halo)
        wide = gather_halo(wide, "fx", 0, halo).astype(jnp.float32)
        field = jnp.einsum("gox,xyz->goyz", table_x, wide, precision=exact)
        field = jnp.einsum("goy,gxyz->gxoz", table_y, field, precision=exact)
        blurred = jnp.einsum("goz,gxyz->gxyo", table_z, field, precision=exact)
        ratio = masked / blurred
        field = jnp.einsum("goz,gxyo->gxyz", table_z, ratio, precision=exact)
        field = jnp.einsum("goy,gxoz->gxyz", table_y, field, precision=exact)
        field = jnp.einsum("gox,goyz->xyz", table_x, field, precision=exact)
        below, above = swap_fixed(field[:halo], field[cells_x + halo :], "fx")
        field = add_edges(field[halo : cells_x + halo], below, above, 0)
        below, above = swap_fixed(field[:, :halo], field[:, cells_y + halo :], "fy")
        field = add_edges(field[:, halo : cells_y + halo], below, above, 1)
        moving = pack_fixed(field)
        correction = unpack_fixed(moving)
        for _ in range(groups - 1):
            moving = lax.ppermute(moving, "view", swap)
            correction = correction + unpack_fixed(moving)
        joined = joined * (correction + 0.5) / lower_part
    return joined


def solution(mesh):
    return jax.shard_map(
        body,
        mesh=mesh,
        in_specs=(
            P("fx", "fy", None),
            P("view", "fx", "fy", None),
            P("view", None, None),
            P("view", None, None),
            P("view", None, None),
        ),
        out_specs=P("fx", "fy", None),
        check_vma=False,
    )
```

```python
import functools

import jax
import jax.numpy as jnp
from jax import lax
from jax.experimental import pallas as pl
from jax.experimental.pallas import tpu as pltpu
from jax.sharding import PartitionSpec as P

ITERS = 2
LANES = 128
OUTER_FIRST, OUTER_LAST = (1, 0), (0, 1)
VMEM = pl.BlockSpec(memory_space=pltpu.VMEM)


def swap_edges(to_below, to_above, axis, order):
    peers = lax.axis_size(axis)
    even = lax.axis_index(axis) % 2 == 0

    def pairs(start):
        out = []
        for i in range(start, peers - 1, 2):
            out += [(i, i + 1), (i + 1, i)]
        return out

    parts = [jnp.where(even, to_above, to_below), jnp.where(even, to_below, to_above)]
    for turn in order:
        parts[turn] = lax.ppermute(parts[turn], axis, pairs(turn))
    first, second = parts
    if order == OUTER_FIRST:
        odd = jnp.logical_not(even)
        return jnp.where(odd, first, second), jnp.where(odd, second, first)
    return jnp.where(even, second, first), jnp.where(even, first, second)


def gather_halo(array, axis, dim, width, order):
    length = array.shape[dim]
    before, after = swap_edges(
        lax.slice_in_dim(array, 0, width, axis=dim),
        lax.slice_in_dim(array, length - width, length, axis=dim),
        axis,
        order,
    )
    return jnp.concatenate([before, array, after], axis=dim)


def add_edges(centre, below, above, dim):
    length, width = centre.shape[dim], below.shape[dim]
    zero = jnp.zeros((), centre.dtype)
    low = [(0, 0, 0)] * centre.ndim
    low[dim] = (0, length - width, 0)
    high = [(0, 0, 0)] * centre.ndim
    high[dim] = (length - width, 0, 0)
    return centre + lax.pad(below, zero, low) + lax.pad(above, zero, high)


def pack_fixed(values):
    top = jnp.max(jnp.abs(values), axis=1, keepdims=True)
    level = jnp.ceil(4.0 * jnp.log2(jnp.maximum(top, 1e-30)) + 0.01)
    scale = 32700.0 * jnp.exp2(-0.25 * level)
    fixed = jnp.round(values * scale).astype(jnp.int16)
    return jnp.concatenate([fixed, level.astype(jnp.int16)], axis=1)


def unpack_fixed(packed):
    step = jnp.exp2(0.25 * packed[:, -1:].astype(jnp.float32)) * (1.0 / 32700.0)
    return packed[:, :-1].astype(jnp.float32) * step


def swap_fixed(to_below, to_above, axis, order):
    below, above = swap_edges(pack_fixed(to_below), pack_fixed(to_above), axis, order)
    return unpack_fixed(below), unpack_fixed(above)


def table_kernel(taps, halo, psf, table_x, table_y, table_z):
    radius = (taps - 1) // 2
    depth = table_z.shape[1]
    for k in range(psf.shape[0]):
        rows = psf[k]
        rows = rows / jnp.sum(rows, axis=1, keepdims=True)
        for axis, table in ((0, table_x), (1, table_y)):
            _, cells, wide = table.shape
            base = jnp.broadcast_to(pltpu.roll(rows[axis : axis + 1], halo - radius, 1), (cells, LANES))
            table[k] = pltpu.roll(base, 0, 1, stride=1, stride_axis=0)[:, :wide]
        base = jnp.broadcast_to(pltpu.roll(rows[2:3], depth - radius, 1), (depth, depth))
        turned = pltpu.roll(base, 0, 1, stride=1, stride_axis=0)
        gap = lax.broadcasted_iota(jnp.int32, (depth, depth), 1) - lax.broadcasted_iota(
            jnp.int32, (depth, depth), 0
        )
        table_z[k] = jnp.where((gap >= -radius) & (gap <= radius), turned, 0.0)


def band(weights, rows, cols, shift):
    taps = weights.shape[-1]
    gap = (
        jnp.arange(cols, dtype=jnp.int32)[None, :]
        - jnp.arange(rows, dtype=jnp.int32)[:, None]
        + shift
    )
    picks = (gap[:, :, None] == jnp.arange(taps, dtype=jnp.int32)).astype(jnp.float32)
    return jnp.einsum("oit,gt->goi", picks, weights, precision=lax.Precision.HIGHEST)


def block_sums(weights, axis, cells):
    blocks = lax.axis_size(axis)
    taps = weights.shape[-1]
    place = lax.axis_index(axis) * cells + jnp.arange(cells, dtype=jnp.int32)
    source = place[:, None] - jnp.arange(taps, dtype=jnp.int32)[None, :] + (taps - 1) // 2
    first = jnp.arange(blocks, dtype=jnp.int32)[:, None, None] * cells
    picks = ((source[None] >= first) & (source[None] < first + cells)).astype(jnp.float32)
    return jnp.einsum("bot,gt->ogb", picks, weights, precision=lax.Precision.HIGHEST)


def weight_of(kern, low, span, cells_x, cells_y, depth):
    views = kern.shape[0]
    taps = kern.shape[-1]
    sums_x = block_sums(kern[:, 0], "fx", cells_x)
    sums_y = block_sums(kern[:, 1], "fy", cells_y)
    levels = jnp.arange(depth, dtype=jnp.int32)
    inside = (levels >= low[..., None]) & (levels < (low + span)[..., None])
    table_z = band(kern[:, 2], depth, depth, (taps - 1) // 2)
    sums_z = jnp.einsum(
        "gxyi,gio->gxyo", inside.astype(jnp.float32), table_z, precision=lax.Precision.HIGHEST
    )
    plane = sums_x[:, None, :, :, None] * sums_y[None, :, :, None, :]
    plane = plane.reshape(cells_x, cells_y, -1)
    return jnp.einsum(
        "xym,mz->xyz", plane, sums_z.reshape(-1, depth), precision=lax.Precision.HIGHEST
    )


def body(estimate, images, psf, cover_lo, cover_len):
    group, cells_x, cells_y, depth = images.shape
    taps = psf.shape[-1]
    radius = (taps - 1) // 2
    halo = min(-(-radius // 16) * 16, cells_x, cells_y)
    exact = lax.Precision.HIGH
    groups = lax.axis_size("view")
    swap = [(i, (i + 1) % groups) for i in range(groups)]

    start = gather_halo(estimate.astype(jnp.bfloat16), "fy", 1, halo, OUTER_FIRST)
    start = gather_halo(start, "fx", 0, halo, OUTER_LAST)
    start, psf_late, lo_late, len_late = lax.optimization_barrier((start, psf, cover_lo, cover_len))
    kern = psf_late / jnp.sum(psf_late, axis=-1, keepdims=True)
    pack = jnp.concatenate(
        [kern.reshape(-1), lo_late.reshape(-1).astype(jnp.float32), len_late.reshape(-1).astype(jnp.float32)]
    )
    packs = [pack]
    for _ in range(groups - 1):
        packs.append(lax.ppermute(packs[-1], "view", swap))
    packs = jnp.stack(packs)
    all_kern = packs[:, : kern.size].reshape((-1,) + kern.shape[1:])
    cells = cover_lo.size
    all_low = packs[:, kern.size : kern.size + cells].astype(jnp.int32).reshape((-1,) + cover_lo.shape[1:])
    all_span = packs[:, kern.size + cells :].astype(jnp.int32).reshape((-1,) + cover_len.shape[1:])
    lower_part = weight_of(all_kern, all_low, all_span, cells_x, cells_y, depth) + 0.5

    block_x, block_y = lax.axis_index("fx"), lax.axis_index("fy")
    low = lax.dynamic_slice(cover_lo, (0, block_x, block_y), (group, 1, 1))[..., None]
    span = lax.dynamic_slice(cover_len, (0, block_x, block_y), (group, 1, 1))[..., None]
    levels = jnp.arange(depth, dtype=jnp.int32)
    own = (levels >= low) & (levels < low + span)
    masked = jnp.where(own, images, jnp.zeros_like(images)).astype(jnp.float32)

    padded = jnp.pad(psf, ((0, 0), (0, 0), (0, LANES - taps)))
    shape = functools.partial(jax.ShapeDtypeStruct, dtype=jnp.float32)
    table_x, table_y, table_z = pl.pallas_call(
        functools.partial(table_kernel, taps, halo),
        out_shape=[
            shape((group, cells_x, cells_x + 2 * halo)),
            shape((group, cells_y, cells_y + 2 * halo)),
            shape((group, depth, depth)),
        ],
        in_specs=[VMEM],
        out_specs=[VMEM] * 3,
    )(padded)

    joined = estimate
    for step in range(ITERS):
        wide = start
        if step > 0:
            wide = gather_halo(joined.astype(jnp.bfloat16), "fy", 1, halo, OUTER_FIRST)
            wide = gather_halo(wide, "fx", 0, halo, OUTER_LAST)
        wide = wide.astype(jnp.float32)
        field = jnp.einsum("gox,xyz->goyz", table_x, wide, precision=exact)
        field = jnp.einsum("goy,gxyz->gxoz", table_y, field, precision=exact)
        blurred = jnp.einsum("goz,gxyz->gxyo", table_z, field, precision=exact)
        ratio = masked / blurred
        field = jnp.einsum("goz,gxyo->gxyz", table_z, ratio, precision=exact)
        field = jnp.einsum("goy,gxoz->gxyz", table_y, field, precision=exact)
        field = jnp.einsum("gox,goyz->xyz", table_x, field, precision=exact)
        below, above = swap_fixed(field[:halo], field[cells_x + halo :], "fx", OUTER_LAST)
        field = add_edges(field[halo : cells_x + halo], below, above, 0)
        below, above = swap_fixed(field[:, :halo], field[:, cells_y + halo :], "fy", OUTER_FIRST)
        field = add_edges(field[:, halo : cells_y + halo], below, above, 1)
        moving = pack_fixed(field)
        correction = unpack_fixed(moving)
        for _ in range(groups - 1):
            moving = lax.ppermute(moving, "view", swap)
            correction = correction + unpack_fixed(moving)
        joined = joined * (correction + 0.5) / lower_part
    return joined


def solution(mesh):
    return jax.shard_map(
        body,
        mesh=mesh,
        in_specs=(
            P("fx", "fy", None),
            P("view", "fx", "fy", None),
            P("view", None, None),
            P("view", None, None),
            P("view", None, None),
        ),
        out_specs=P("fx", "fy", None),
        check_vma=False,
    )
```

```python
import functools

import jax
import jax.numpy as jnp
from jax import lax
from jax.experimental import pallas as pl
from jax.experimental.pallas import tpu as pltpu
from jax.sharding import PartitionSpec as P

ITERS = 2
LANES = 128
VMEM = pl.BlockSpec(memory_space=pltpu.VMEM)


def swap_edges(to_below, to_above, axis, late=()):
    peers = lax.axis_size(axis)
    even = lax.axis_index(axis) % 2 == 0

    def pairs(start):
        out = []
        for i in range(start, peers - 1, 2):
            out += [(i, i + 1), (i + 1, i)]
        return out

    first = lax.ppermute(jnp.where(even, to_above, to_below), axis, pairs(0))
    second = lax.ppermute(jnp.where(even, to_below, to_above), axis, pairs(1))
    if late:
        first, *late = lax.optimization_barrier((first, *late))
    odd = jnp.logical_not(even)
    return jnp.where(odd, first, second), jnp.where(odd, second, first), late


def gather_halo(array, axis, dim, width):
    length = array.shape[dim]
    before, after, _ = swap_edges(
        lax.slice_in_dim(array, 0, width, axis=dim),
        lax.slice_in_dim(array, length - width, length, axis=dim),
        axis,
    )
    return jnp.concatenate([before, array, after], axis=dim)


def add_edges(centre, below, above, dim):
    length, width = centre.shape[dim], below.shape[dim]
    zero = jnp.zeros((), centre.dtype)
    low = [(0, 0, 0)] * centre.ndim
    low[dim] = (0, length - width, 0)
    high = [(0, 0, 0)] * centre.ndim
    high[dim] = (length - width, 0, 0)
    return centre + lax.pad(below, zero, low) + lax.pad(above, zero, high)


def pack_fixed(values):
    top = jnp.max(jnp.abs(values), axis=1, keepdims=True)
    level = jnp.ceil(4.0 * jnp.log2(jnp.maximum(top, 1e-30)) + 0.01)
    scale = 32700.0 * jnp.exp2(-0.25 * level)
    fixed = jnp.round(values * scale).astype(jnp.int16)
    return jnp.concatenate([fixed, level.astype(jnp.int16)], axis=1)


def unpack_fixed(packed):
    step = jnp.exp2(0.25 * packed[:, -1:].astype(jnp.float32)) * (1.0 / 32700.0)
    return packed[:, :-1].astype(jnp.float32) * step


def swap_fixed(to_below, to_above, axis, late=()):
    below, above, late = swap_edges(pack_fixed(to_below), pack_fixed(to_above), axis, late)
    return unpack_fixed(below), unpack_fixed(above), late


def table_kernel(taps, halo, psf, table_x, table_y, table_z):
    radius = (taps - 1) // 2
    depth = table_z.shape[1]
    for k in range(psf.shape[0]):
        rows = psf[k]
        rows = rows / jnp.sum(rows, axis=1, keepdims=True)
        for axis, table in ((0, table_x), (1, table_y)):
            _, cells, wide = table.shape
            base = jnp.broadcast_to(pltpu.roll(rows[axis : axis + 1], halo - radius, 1), (cells, LANES))
            table[k] = pltpu.roll(base, 0, 1, stride=1, stride_axis=0)[:, :wide]
        base = jnp.broadcast_to(pltpu.roll(rows[2:3], depth - radius, 1), (depth, depth))
        turned = pltpu.roll(base, 0, 1, stride=1, stride_axis=0)
        gap = lax.broadcasted_iota(jnp.int32, (depth, depth), 1) - lax.broadcasted_iota(
            jnp.int32, (depth, depth), 0
        )
        table_z[k] = jnp.where((gap >= -radius) & (gap <= radius), turned, 0.0)


def band(weights, rows, cols, shift):
    taps = weights.shape[-1]
    gap = (
        jnp.arange(cols, dtype=jnp.int32)[None, :]
        - jnp.arange(rows, dtype=jnp.int32)[:, None]
        + shift
    )
    picks = (gap[:, :, None] == jnp.arange(taps, dtype=jnp.int32)).astype(jnp.float32)
    return jnp.einsum("oit,gt->goi", picks, weights, precision=lax.Precision.HIGHEST)


def block_sums(weights, axis, cells):
    blocks = lax.axis_size(axis)
    taps = weights.shape[-1]
    place = lax.axis_index(axis) * cells + jnp.arange(cells, dtype=jnp.int32)
    source = place[:, None] - jnp.arange(taps, dtype=jnp.int32)[None, :] + (taps - 1) // 2
    first = jnp.arange(blocks, dtype=jnp.int32)[:, None, None] * cells
    picks = ((source[None] >= first) & (source[None] < first + cells)).astype(jnp.float32)
    return jnp.einsum("bot,gt->ogb", picks, weights, precision=lax.Precision.HIGHEST)


def weight_of(kern, low, span, cells_x, cells_y, depth):
    views = kern.shape[0]
    taps = kern.shape[-1]
    sums_x = block_sums(kern[:, 0], "fx", cells_x)
    sums_y = block_sums(kern[:, 1], "fy", cells_y)
    levels = jnp.arange(depth, dtype=jnp.int32)
    inside = (levels >= low[..., None]) & (levels < (low + span)[..., None])
    table_z = band(kern[:, 2], depth, depth, (taps - 1) // 2)
    sums_z = jnp.einsum(
        "gxyi,gio->gxyo", inside.astype(jnp.float32), table_z, precision=lax.Precision.HIGHEST
    )
    plane = sums_x[:, None, :, :, None] * sums_y[None, :, :, None, :]
    plane = plane.reshape(cells_x, cells_y, -1)
    return jnp.einsum(
        "xym,mz->xyz", plane, sums_z.reshape(-1, depth), precision=lax.Precision.HIGHEST
    )


def view_tables(psf, cover_lo, cover_len, swap):
    kern = psf / jnp.sum(psf, axis=-1, keepdims=True)
    pack = jnp.concatenate(
        [kern.reshape(-1), cover_lo.reshape(-1).astype(jnp.float32), cover_len.reshape(-1).astype(jnp.float32)]
    )
    packs = [pack]
    for _ in range(len(swap) - 1):
        packs.append(lax.ppermute(packs[-1], "view", swap))
    packs = jnp.stack(packs)
    all_kern = packs[:, : kern.size].reshape((-1,) + kern.shape[1:])
    cells = cover_lo.size
    all_low = packs[:, kern.size : kern.size + cells].astype(jnp.int32).reshape((-1,) + cover_lo.shape[1:])
    all_span = packs[:, kern.size + cells :].astype(jnp.int32).reshape((-1,) + cover_len.shape[1:])
    return all_kern, all_low, all_span


def body(estimate, images, psf, cover_lo, cover_len):
    group, cells_x, cells_y, depth = images.shape
    taps = psf.shape[-1]
    radius = (taps - 1) // 2
    halo = min(-(-radius // 16) * 16, cells_x, cells_y)
    exact = lax.Precision.HIGH
    groups = lax.axis_size("view")
    swap = [(i, (i + 1) % groups) for i in range(groups)]

    start = gather_halo(estimate.astype(jnp.bfloat16), "fy", 1, halo)
    start = gather_halo(start, "fx", 0, halo)
    block_x, block_y = lax.axis_index("fx"), lax.axis_index("fy")
    low = lax.dynamic_slice(cover_lo, (0, block_x, block_y), (group, 1, 1))[..., None]
    span = lax.dynamic_slice(cover_len, (0, block_x, block_y), (group, 1, 1))[..., None]
    levels = jnp.arange(depth, dtype=jnp.int32)
    own = (levels >= low) & (levels < low + span)
    masked = jnp.where(own, images, jnp.zeros_like(images)).astype(jnp.float32)

    padded = jnp.pad(psf, ((0, 0), (0, 0), (0, LANES - taps)))
    shape = functools.partial(jax.ShapeDtypeStruct, dtype=jnp.float32)
    table_x, table_y, table_z = pl.pallas_call(
        functools.partial(table_kernel, taps, halo),
        out_shape=[
            shape((group, cells_x, cells_x + 2 * halo)),
            shape((group, cells_y, cells_y + 2 * halo)),
            shape((group, depth, depth)),
        ],
        in_specs=[VMEM],
        out_specs=[VMEM] * 3,
    )(padded)

    joined = estimate
    for step in range(ITERS):
        wide = start
        if step > 0:
            wide = gather_halo(joined.astype(jnp.bfloat16), "fy", 1, halo)
            wide = gather_halo(wide, "fx", 0, halo)
        wide = wide.astype(jnp.float32)
        field = jnp.einsum("gox,xyz->goyz", table_x, wide, precision=exact)
        field = jnp.einsum("goy,gxyz->gxoz", table_y, field, precision=exact)
        blurred = jnp.einsum("goz,gxyz->gxyo", table_z, field, precision=exact)
        ratio = masked / blurred
        field = jnp.einsum("goz,gxyo->gxyz", table_z, ratio, precision=exact)
        field = jnp.einsum("goy,gxoz->gxyz", table_y, field, precision=exact)
        field = jnp.einsum("gox,goyz->xyz", table_x, field, precision=exact)
        late = (psf, cover_lo, cover_len) if step == 0 else ()
        below, above, late = swap_fixed(field[:halo], field[cells_x + halo :], "fx", late)
        if step == 0:
            lower_part = weight_of(*view_tables(*late, swap), cells_x, cells_y, depth) + 0.5
        field = add_edges(field[halo : cells_x + halo], below, above, 0)
        below, above, _ = swap_fixed(field[:, :halo], field[:, cells_y + halo :], "fy")
        field = add_edges(field[:, halo : cells_y + halo], below, above, 1)
        moving = pack_fixed(field)
        correction = unpack_fixed(moving)
        for _ in range(groups - 1):
            moving = lax.ppermute(moving, "view", swap)
            correction = correction + unpack_fixed(moving)
        joined = joined * (correction + 0.5) / lower_part
    return joined


def solution(mesh):
    return jax.shard_map(
        body,
        mesh=mesh,
        in_specs=(
            P("fx", "fy", None),
            P("view", "fx", "fy", None),
            P("view", None, None),
            P("view", None, None),
            P("view", None, None),
        ),
        out_specs=P("fx", "fy", None),
        check_vma=False,
    )
```

```python
import functools

import jax
import jax.numpy as jnp
from jax import lax
from jax.experimental import pallas as pl
from jax.experimental.pallas import tpu as pltpu
from jax.sharding import PartitionSpec as P

ITERS = 2
LANES = 128
VMEM = pl.BlockSpec(memory_space=pltpu.VMEM)


def swap_edges(to_below, to_above, axis, late=()):
    peers = lax.axis_size(axis)
    even = lax.axis_index(axis) % 2 == 0

    def pairs(start):
        out = []
        for i in range(start, peers - 1, 2):
            out += [(i, i + 1), (i + 1, i)]
        return out

    first = lax.ppermute(jnp.where(even, to_above, to_below), axis, pairs(0))
    second = lax.ppermute(jnp.where(even, to_below, to_above), axis, pairs(1))
    if late:
        first, *late = lax.optimization_barrier((first, *late))
    if axis == "fx":
        return jnp.where(even, second, first), jnp.where(even, first, second), late
    odd = jnp.logical_not(even)
    return jnp.where(odd, first, second), jnp.where(odd, second, first), late


def gather_halo(array, axis, dim, width):
    length = array.shape[dim]
    before, after, _ = swap_edges(
        lax.slice_in_dim(array, 0, width, axis=dim),
        lax.slice_in_dim(array, length - width, length, axis=dim),
        axis,
    )
    return jnp.concatenate([before, array, after], axis=dim)


def add_edges(centre, below, above, dim):
    length, width = centre.shape[dim], below.shape[dim]
    zero = jnp.zeros((), centre.dtype)
    low = [(0, 0, 0)] * centre.ndim
    low[dim] = (0, length - width, 0)
    high = [(0, 0, 0)] * centre.ndim
    high[dim] = (length - width, 0, 0)
    return centre + lax.pad(below, zero, low) + lax.pad(above, zero, high)


def pack_fixed(values):
    top = jnp.max(jnp.abs(values), axis=1, keepdims=True)
    level = jnp.ceil(4.0 * jnp.log2(jnp.maximum(top, 1e-30)) + 0.01)
    scale = 32700.0 * jnp.exp2(-0.25 * level)
    fixed = jnp.round(values * scale).astype(jnp.int16)
    return jnp.concatenate([fixed, level.astype(jnp.int16)], axis=1)


def unpack_fixed(packed):
    step = jnp.exp2(0.25 * packed[:, -1:].astype(jnp.float32)) * (1.0 / 32700.0)
    return packed[:, :-1].astype(jnp.float32) * step


def swap_fixed(to_below, to_above, axis, late=()):
    below, above, late = swap_edges(pack_fixed(to_below), pack_fixed(to_above), axis, late)
    return unpack_fixed(below), unpack_fixed(above), late


def table_kernel(taps, halo, psf, table_x, table_y, table_z):
    radius = (taps - 1) // 2
    depth = table_z.shape[1]
    for k in range(psf.shape[0]):
        rows = psf[k]
        rows = rows / jnp.sum(rows, axis=1, keepdims=True)
        for axis, table in ((0, table_x), (1, table_y)):
            _, cells, wide = table.shape
            base = jnp.broadcast_to(pltpu.roll(rows[axis : axis + 1], halo - radius, 1), (cells, LANES))
            table[k] = pltpu.roll(base, 0, 1, stride=1, stride_axis=0)[:, :wide]
        base = jnp.broadcast_to(pltpu.roll(rows[2:3], depth - radius, 1), (depth, depth))
        turned = pltpu.roll(base, 0, 1, stride=1, stride_axis=0)
        gap = lax.broadcasted_iota(jnp.int32, (depth, depth), 1) - lax.broadcasted_iota(
            jnp.int32, (depth, depth), 0
        )
        table_z[k] = jnp.where((gap >= -radius) & (gap <= radius), turned, 0.0)


def block_sums(weights, axis, cells):
    blocks = lax.axis_size(axis)
    taps = weights.shape[-1]
    place = lax.axis_index(axis) * cells + jnp.arange(cells, dtype=jnp.int32)
    source = place[:, None] - jnp.arange(taps, dtype=jnp.int32)[None, :] + (taps - 1) // 2
    first = jnp.arange(blocks, dtype=jnp.int32)[:, None, None] * cells
    picks = ((source[None] >= first) & (source[None] < first + cells)).astype(jnp.float32)
    return jnp.einsum("bot,gt->ogb", picks, weights, precision=lax.Precision.HIGHEST)


def weight_of(kern, low, span, cells_x, cells_y, depth):
    views = kern.shape[0]
    taps = kern.shape[-1]
    sums_x = block_sums(kern[:, 0], "fx", cells_x)
    sums_y = block_sums(kern[:, 1], "fy", cells_y)
    shift = jnp.arange(depth, dtype=jnp.int32)[None, :] - jnp.arange(taps, dtype=jnp.int32)[:, None]
    source = (shift + (taps - 1) // 2)[:, None, None, None, :]
    inside = (source >= low[None, ..., None]) & (source < (low + span)[None, ..., None])
    sums_z = jnp.sum(jnp.where(inside, kern[:, 2].T[:, :, None, None, None], 0.0), axis=0)
    plane = sums_x[:, None, :, :, None] * sums_y[None, :, :, None, :]
    plane = plane.reshape(cells_x, cells_y, -1)
    return jnp.einsum(
        "xym,mz->xyz", plane, sums_z.reshape(-1, depth), precision=lax.Precision.HIGHEST
    )


def view_tables(psf, cover_lo, cover_len, swap):
    kern = psf / jnp.sum(psf, axis=-1, keepdims=True)
    pack = jnp.concatenate(
        [kern.reshape(-1), cover_lo.reshape(-1).astype(jnp.float32), cover_len.reshape(-1).astype(jnp.float32)]
    )
    packs = [pack]
    for _ in range(len(swap) - 1):
        packs.append(lax.ppermute(packs[-1], "view", swap))
    packs = jnp.stack(packs)
    all_kern = packs[:, : kern.size].reshape((-1,) + kern.shape[1:])
    cells = cover_lo.size
    all_low = packs[:, kern.size : kern.size + cells].astype(jnp.int32).reshape((-1,) + cover_lo.shape[1:])
    all_span = packs[:, kern.size + cells :].astype(jnp.int32).reshape((-1,) + cover_len.shape[1:])
    return all_kern, all_low, all_span


def body(estimate, images, psf, cover_lo, cover_len):
    group, cells_x, cells_y, depth = images.shape
    taps = psf.shape[-1]
    radius = (taps - 1) // 2
    halo = min(-(-radius // 16) * 16, cells_x, cells_y)
    exact = lax.Precision.HIGH
    groups = lax.axis_size("view")
    swap = [(i, (i + 1) % groups) for i in range(groups)]

    start = gather_halo(estimate.astype(jnp.bfloat16), "fy", 1, halo)
    start = gather_halo(start, "fx", 0, halo)
    block_x, block_y = lax.axis_index("fx"), lax.axis_index("fy")
    low = lax.dynamic_slice(cover_lo, (0, block_x, block_y), (group, 1, 1))[..., None]
    span = lax.dynamic_slice(cover_len, (0, block_x, block_y), (group, 1, 1))[..., None]
    levels = jnp.arange(depth, dtype=jnp.int32)
    own = (levels >= low) & (levels < low + span)
    masked = jnp.where(own, images, jnp.zeros_like(images)).astype(jnp.float32)

    padded = jnp.pad(psf, ((0, 0), (0, 0), (0, LANES - taps)))
    shape = functools.partial(jax.ShapeDtypeStruct, dtype=jnp.float32)
    table_x, table_y, table_z = pl.pallas_call(
        functools.partial(table_kernel, taps, halo),
        out_shape=[
            shape((group, cells_x, cells_x + 2 * halo)),
            shape((group, cells_y, cells_y + 2 * halo)),
            shape((group, depth, depth)),
        ],
        in_specs=[VMEM],
        out_specs=[VMEM] * 3,
    )(padded)

    joined = estimate
    for step in range(ITERS):
        wide = start
        if step > 0:
            wide = gather_halo(joined.astype(jnp.bfloat16), "fy", 1, halo)
            wide = gather_halo(wide, "fx", 0, halo)
        wide = wide.astype(jnp.float32)
        field = jnp.einsum("gox,xyz->goyz", table_x, wide, precision=exact)
        field = jnp.einsum("goy,gxyz->gxoz", table_y, field, precision=exact)
        blurred = jnp.einsum("goz,gxyz->gxyo", table_z, field, precision=exact)
        ratio = masked / blurred
        field = jnp.einsum("goz,gxyo->gxyz", table_z, ratio, precision=exact)
        field = jnp.einsum("goy,gxoz->gxyz", table_y, field, precision=exact)
        field = jnp.einsum("gox,goyz->xyz", table_x, field, precision=exact)
        late = (psf, cover_lo, cover_len) if step == 0 else ()
        below, above, late = swap_fixed(field[:halo], field[cells_x + halo :], "fx", late)
        if step == 0:
            lower_part = weight_of(*view_tables(*late, swap), cells_x, cells_y, depth) + 0.5
        field = add_edges(field[halo : cells_x + halo], below, above, 0)
        below, above, _ = swap_fixed(field[:, :halo], field[:, cells_y + halo :], "fy")
        field = add_edges(field[:, halo : cells_y + halo], below, above, 1)
        moving = pack_fixed(field)
        correction = unpack_fixed(moving)
        for _ in range(groups - 1):
            moving = lax.ppermute(moving, "view", swap)
            correction = correction + unpack_fixed(moving)
        joined = joined * (correction + 0.5) / lower_part
    return joined


def solution(mesh):
    return jax.shard_map(
        body,
        mesh=mesh,
        in_specs=(
            P("fx", "fy", None),
            P("view", "fx", "fy", None),
            P("view", None, None),
            P("view", None, None),
            P("view", None, None),
        ),
        out_specs=P("fx", "fy", None),
        check_vma=False,
    )
```

```python
import functools

import jax
import jax.numpy as jnp
from jax import lax
from jax.experimental import pallas as pl
from jax.experimental.pallas import tpu as pltpu
from jax.sharding import PartitionSpec as P

ITERS = 2
LANES = 128
VMEM = pl.BlockSpec(memory_space=pltpu.VMEM)


def swap_edges(to_below, to_above, axis, late=()):
    peers = lax.axis_size(axis)
    even = lax.axis_index(axis) % 2 == 0

    def pairs(start):
        out = []
        for i in range(start, peers - 1, 2):
            out += [(i, i + 1), (i + 1, i)]
        return out

    first = lax.ppermute(jnp.where(even, to_above, to_below), axis, pairs(0))
    second = lax.ppermute(jnp.where(even, to_below, to_above), axis, pairs(1))
    if late:
        first, *late = lax.optimization_barrier((first, *late))
    if axis == "fx":
        return jnp.where(even, second, first), jnp.where(even, first, second), late
    odd = jnp.logical_not(even)
    return jnp.where(odd, first, second), jnp.where(odd, second, first), late


def gather_halo(array, axis, dim, width):
    length = array.shape[dim]
    before, after, _ = swap_edges(
        lax.slice_in_dim(array, 0, width, axis=dim),
        lax.slice_in_dim(array, length - width, length, axis=dim),
        axis,
    )
    return jnp.concatenate([before, array, after], axis=dim)


def add_edges(centre, below, above, dim):
    length, width = centre.shape[dim], below.shape[dim]
    zero = jnp.zeros((), centre.dtype)
    low = [(0, 0, 0)] * centre.ndim
    low[dim] = (0, length - width, 0)
    high = [(0, 0, 0)] * centre.ndim
    high[dim] = (length - width, 0, 0)
    return centre + lax.pad(below, zero, low) + lax.pad(above, zero, high)


def pack_fixed(values):
    top = jnp.max(jnp.abs(values), axis=1, keepdims=True)
    level = jnp.ceil(4.0 * jnp.log2(jnp.maximum(top, 1e-30)) + 0.01)
    scale = 32700.0 * jnp.exp2(-0.25 * level)
    fixed = jnp.round(values * scale).astype(jnp.int16)
    return jnp.concatenate([fixed, level.astype(jnp.int16)], axis=1)


def unpack_fixed(packed):
    step = jnp.exp2(0.25 * packed[:, -1:].astype(jnp.float32)) * (1.0 / 32700.0)
    return packed[:, :-1].astype(jnp.float32) * step


def swap_fixed(to_below, to_above, axis, late=()):
    below, above, late = swap_edges(pack_fixed(to_below), pack_fixed(to_above), axis, late)
    return unpack_fixed(below), unpack_fixed(above), late


def table_kernel(taps, halo, psf, table_x, table_y, table_z):
    radius = (taps - 1) // 2
    depth = table_z.shape[1]
    for k in range(psf.shape[0]):
        rows = psf[k]
        rows = rows / jnp.sum(rows, axis=1, keepdims=True)
        for axis, table in ((0, table_x), (1, table_y)):
            _, cells, wide = table.shape
            base = jnp.broadcast_to(pltpu.roll(rows[axis : axis + 1], halo - radius, 1), (cells, LANES))
            table[k] = pltpu.roll(base, 0, 1, stride=1, stride_axis=0)[:, :wide]
        base = jnp.broadcast_to(pltpu.roll(rows[2:3], depth - radius, 1), (depth, depth))
        turned = pltpu.roll(base, 0, 1, stride=1, stride_axis=0)
        gap = lax.broadcasted_iota(jnp.int32, (depth, depth), 1) - lax.broadcasted_iota(
            jnp.int32, (depth, depth), 0
        )
        table_z[k] = jnp.where((gap >= -radius) & (gap <= radius), turned, 0.0)


def block_sums(weights, axis, cells):
    blocks = lax.axis_size(axis)
    taps = weights.shape[-1]
    place = lax.axis_index(axis) * cells + jnp.arange(cells, dtype=jnp.int32)
    source = place[:, None] - jnp.arange(taps, dtype=jnp.int32)[None, :] + (taps - 1) // 2
    first = jnp.arange(blocks, dtype=jnp.int32)[:, None, None] * cells
    picks = ((source[None] >= first) & (source[None] < first + cells)).astype(jnp.float32)
    return jnp.einsum("bot,gt->ogb", picks, weights, precision=lax.Precision.HIGHEST)


def weight_of(kern, low, span, cells_x, cells_y, depth):
    views = kern.shape[0]
    taps = kern.shape[-1]
    sums_x = block_sums(kern[:, 0], "fx", cells_x)
    sums_y = block_sums(kern[:, 1], "fy", cells_y)
    shift = jnp.arange(depth, dtype=jnp.int32)[None, :] - jnp.arange(taps, dtype=jnp.int32)[:, None]
    source = (shift + (taps - 1) // 2)[:, None, None, None, :]
    inside = (source >= low[None, ..., None]) & (source < (low + span)[None, ..., None])
    sums_z = jnp.sum(jnp.where(inside, kern[:, 2].T[:, :, None, None, None], 0.0), axis=0)
    plane = sums_x[:, None, :, :, None] * sums_y[None, :, :, None, :]
    plane = plane.reshape(cells_x, cells_y, -1)
    return jnp.einsum(
        "xym,mz->xyz", plane, sums_z.reshape(-1, depth), precision=lax.Precision.HIGHEST
    )


def view_tables(psf, cover_lo, cover_len, swap):
    kern = psf / jnp.sum(psf, axis=-1, keepdims=True)
    pack = jnp.concatenate(
        [kern.reshape(-1), cover_lo.reshape(-1).astype(jnp.float32), cover_len.reshape(-1).astype(jnp.float32)]
    )
    packs = [pack]
    for _ in range(len(swap) - 1):
        packs.append(lax.ppermute(packs[-1], "view", swap))
    packs = jnp.stack(packs)
    all_kern = packs[:, : kern.size].reshape((-1,) + kern.shape[1:])
    cells = cover_lo.size
    all_low = packs[:, kern.size : kern.size + cells].astype(jnp.int32).reshape((-1,) + cover_lo.shape[1:])
    all_span = packs[:, kern.size + cells :].astype(jnp.int32).reshape((-1,) + cover_len.shape[1:])
    return all_kern, all_low, all_span


def body(estimate, images, psf, cover_lo, cover_len):
    group, cells_x, cells_y, depth = images.shape
    taps = psf.shape[-1]
    radius = (taps - 1) // 2
    halo = min(-(-radius // 16) * 16, cells_x, cells_y)
    exact = lax.Precision.HIGH
    groups = lax.axis_size("view")
    swap = [(i, (i + 1) % groups) for i in range(groups)]

    start = gather_halo(estimate.astype(jnp.bfloat16), "fy", 1, halo)
    start = gather_halo(start, "fx", 0, halo)
    block_x, block_y = lax.axis_index("fx"), lax.axis_index("fy")
    low = lax.dynamic_slice(cover_lo, (0, block_x, block_y), (group, 1, 1))[..., None]
    span = lax.dynamic_slice(cover_len, (0, block_x, block_y), (group, 1, 1))[..., None]
    levels = jnp.arange(depth, dtype=jnp.int32)
    own = (levels >= low) & (levels < low + span)
    masked = jnp.where(own, images, jnp.zeros_like(images)).astype(jnp.float32)

    padded = jnp.pad(psf, ((0, 0), (0, 0), (0, LANES - taps)))
    shape = functools.partial(jax.ShapeDtypeStruct, dtype=jnp.float32)
    table_x, table_y, table_z = pl.pallas_call(
        functools.partial(table_kernel, taps, halo),
        out_shape=[
            shape((group, cells_x, cells_x + 2 * halo)),
            shape((group, cells_y, cells_y + 2 * halo)),
            shape((group, depth, depth)),
        ],
        in_specs=[VMEM],
        out_specs=[VMEM] * 3,
    )(padded)

    chunks = 2 if cells_x % 32 == 0 else 1
    start = lax.optimization_barrier(start)
    joined = jnp.split(estimate, chunks, axis=0)
    for step in range(ITERS):
        wide = start
        if step > 0:
            wide = gather_halo(jnp.concatenate(wides, axis=0), "fx", 0, halo)
        wide = wide.astype(jnp.float32)
        field = jnp.einsum("gox,xyz->goyz", table_x, wide, precision=exact)
        field = jnp.einsum("goy,gxyz->gxoz", table_y, field, precision=exact)
        blurred = jnp.einsum("goz,gxyz->gxyo", table_z, field, precision=exact)
        ratio = masked / blurred
        field = jnp.einsum("goz,gxyo->gxyz", table_z, ratio, precision=exact)
        field = jnp.einsum("goy,gxoz->gxyz", table_y, field, precision=exact)
        field = jnp.einsum("gox,goyz->xyz", table_x, field, precision=exact)
        late = (psf, cover_lo, cover_len) if step == 0 else ()
        below, above, late = swap_fixed(field[:halo], field[cells_x + halo :], "fx", late)
        if step == 0:
            weight = weight_of(*view_tables(*late, swap), cells_x, cells_y, depth)
            lower_parts = jnp.split(weight + 0.5, chunks, axis=0)
        field = add_edges(field[halo : cells_x + halo], below, above, 0)
        own, moves = [], []
        for chunk in jnp.split(field, chunks, axis=0):
            low, high = pack_fixed(chunk[:, :halo]), pack_fixed(chunk[:, cells_y + halo :])
            below, above, _ = swap_edges(low, high, "fy")
            if own:
                below, above, _ = lax.optimization_barrier((below, above, own[-1]))
            chunk = chunk[:, halo : cells_y + halo]
            own.append(pack_fixed(add_edges(chunk, unpack_fixed(below), unpack_fixed(above), 1)))
            moves.append([])
            moving = own[-1]
            for _ in range(groups - 1):
                moving = lax.ppermute(moving, "view", swap)
                moves[-1].append(moving)
        wides, ready = [], None
        for at in range(chunks):
            if ready is not None:
                moves[at], _ = lax.optimization_barrier((moves[at], ready))
            correction = sum(map(unpack_fixed, moves[at]), unpack_fixed(own[at]))
            joined[at] = joined[at] * (correction + 0.5) / lower_parts[at]
            ready = joined[at].astype(jnp.bfloat16)
            if step < ITERS - 1:
                wides.append(gather_halo(ready, "fy", 1, halo))
    return jnp.concatenate(joined, axis=0)


def solution(mesh):
    return jax.shard_map(
        body,
        mesh=mesh,
        in_specs=(
            P("fx", "fy", None),
            P("view", "fx", "fy", None),
            P("view", None, None),
            P("view", None, None),
            P("view", None, None),
        ),
        out_specs=P("fx", "fy", None),
        check_vma=False,
    )
```

```python
import functools

import jax
import jax.numpy as jnp
from jax import lax
from jax.experimental import pallas as pl
from jax.experimental.pallas import tpu as pltpu
from jax.sharding import PartitionSpec as P

ITERS = 2
LANES = 128
VMEM = pl.BlockSpec(memory_space=pltpu.VMEM)


def swap_edges(to_below, to_above, axis, late=()):
    peers = lax.axis_size(axis)
    even = lax.axis_index(axis) % 2 == 0

    def pairs(start):
        out = []
        for i in range(start, peers - 1, 2):
            out += [(i, i + 1), (i + 1, i)]
        return out

    first = lax.ppermute(jnp.where(even, to_above, to_below), axis, pairs(0))
    second = lax.ppermute(jnp.where(even, to_below, to_above), axis, pairs(1))
    if late:
        first, *late = lax.optimization_barrier((first, *late))
    if axis == "fx":
        return jnp.where(even, second, first), jnp.where(even, first, second), late
    odd = jnp.logical_not(even)
    return jnp.where(odd, first, second), jnp.where(odd, second, first), late


def gather_halo(array, axis, dim, width):
    length = array.shape[dim]
    before, after, _ = swap_edges(
        lax.slice_in_dim(array, 0, width, axis=dim),
        lax.slice_in_dim(array, length - width, length, axis=dim),
        axis,
    )
    return jnp.concatenate([before, array, after], axis=dim)


def add_edges(centre, below, above, dim):
    length, width = centre.shape[dim], below.shape[dim]
    zero = jnp.zeros((), centre.dtype)
    low = [(0, 0, 0)] * centre.ndim
    low[dim] = (0, length - width, 0)
    high = [(0, 0, 0)] * centre.ndim
    high[dim] = (length - width, 0, 0)
    return centre + lax.pad(below, zero, low) + lax.pad(above, zero, high)


def pack_fixed(values):
    top = jnp.max(jnp.abs(values), axis=1, keepdims=True)
    level = jnp.ceil(4.0 * jnp.log2(jnp.maximum(top, 1e-30)) + 0.01)
    scale = 32700.0 * jnp.exp2(-0.25 * level)
    fixed = jnp.round(values * scale).astype(jnp.int16)
    return jnp.concatenate([fixed, level.astype(jnp.int16)], axis=1)


def unpack_fixed(packed):
    step = jnp.exp2(0.25 * packed[:, -1:].astype(jnp.float32)) * (1.0 / 32700.0)
    return packed[:, :-1].astype(jnp.float32) * step


def swap_fixed(to_below, to_above, axis, late=()):
    below, above, late = swap_edges(pack_fixed(to_below), pack_fixed(to_above), axis, late)
    return unpack_fixed(below), unpack_fixed(above), late


def table_kernel(taps, halo, psf, table_x, table_y, table_z):
    radius = (taps - 1) // 2
    depth = table_z.shape[1]
    for k in range(psf.shape[0]):
        rows = psf[k]
        rows = rows / jnp.sum(rows, axis=1, keepdims=True)
        for axis, table in ((0, table_x), (1, table_y)):
            _, cells, wide = table.shape
            base = jnp.broadcast_to(pltpu.roll(rows[axis : axis + 1], halo - radius, 1), (cells, LANES))
            table[k] = pltpu.roll(base, 0, 1, stride=1, stride_axis=0)[:, :wide]
        base = jnp.broadcast_to(pltpu.roll(rows[2:3], depth - radius, 1), (depth, depth))
        turned = pltpu.roll(base, 0, 1, stride=1, stride_axis=0)
        gap = lax.broadcasted_iota(jnp.int32, (depth, depth), 1) - lax.broadcasted_iota(
            jnp.int32, (depth, depth), 0
        )
        table_z[k] = jnp.where((gap >= -radius) & (gap <= radius), turned, 0.0)


def block_sums(weights, axis, cells):
    blocks = lax.axis_size(axis)
    taps = weights.shape[-1]
    place = lax.axis_index(axis) * cells + jnp.arange(cells, dtype=jnp.int32)
    source = place[:, None] - jnp.arange(taps, dtype=jnp.int32)[None, :] + (taps - 1) // 2
    first = jnp.arange(blocks, dtype=jnp.int32)[:, None, None] * cells
    picks = ((source[None] >= first) & (source[None] < first + cells)).astype(jnp.float32)
    return jnp.einsum("bot,gt->ogb", picks, weights, precision=lax.Precision.HIGHEST)


def weight_of(kern, low, span, cells_x, cells_y, depth):
    views = kern.shape[0]
    taps = kern.shape[-1]
    sums_x = block_sums(kern[:, 0], "fx", cells_x)
    sums_y = block_sums(kern[:, 1], "fy", cells_y)
    shift = jnp.arange(depth, dtype=jnp.int32)[None, :] - jnp.arange(taps, dtype=jnp.int32)[:, None]
    source = (shift + (taps - 1) // 2)[:, None, None, None, :]
    inside = (source >= low[None, ..., None]) & (source < (low + span)[None, ..., None])
    sums_z = jnp.sum(jnp.where(inside, kern[:, 2].T[:, :, None, None, None], 0.0), axis=0)
    plane = sums_x[:, None, :, :, None] * sums_y[None, :, :, None, :]
    plane = plane.reshape(cells_x, cells_y, -1)
    return jnp.einsum(
        "xym,mz->xyz", plane, sums_z.reshape(-1, depth), precision=lax.Precision.HIGHEST
    )


def view_tables(psf, cover_lo, cover_len, swap):
    kern = psf / jnp.sum(psf, axis=-1, keepdims=True)
    pack = jnp.concatenate(
        [kern.reshape(-1), cover_lo.reshape(-1).astype(jnp.float32), cover_len.reshape(-1).astype(jnp.float32)]
    )
    packs = [pack]
    for _ in range(len(swap) - 1):
        packs.append(lax.ppermute(packs[-1], "view", swap))
    packs = jnp.stack(packs)
    all_kern = packs[:, : kern.size].reshape((-1,) + kern.shape[1:])
    cells = cover_lo.size
    all_low = packs[:, kern.size : kern.size + cells].astype(jnp.int32).reshape((-1,) + cover_lo.shape[1:])
    all_span = packs[:, kern.size + cells :].astype(jnp.int32).reshape((-1,) + cover_len.shape[1:])
    return all_kern, all_low, all_span


def body(estimate, images, psf, cover_lo, cover_len):
    group, cells_x, cells_y, depth = images.shape
    taps = psf.shape[-1]
    radius = (taps - 1) // 2
    halo = min(-(-radius // 16) * 16, cells_x, cells_y)
    exact = lax.Precision.HIGH
    groups = lax.axis_size("view")
    swap = [(i, (i + 1) % groups) for i in range(groups)]

    start = gather_halo(estimate.astype(jnp.bfloat16), "fy", 1, halo)
    start = gather_halo(start, "fx", 0, halo)
    block_x, block_y = lax.axis_index("fx"), lax.axis_index("fy")
    low = lax.dynamic_slice(cover_lo, (0, block_x, block_y), (group, 1, 1))[..., None]
    span = lax.dynamic_slice(cover_len, (0, block_x, block_y), (group, 1, 1))[..., None]
    levels = jnp.arange(depth, dtype=jnp.int32)
    own = (levels >= low) & (levels < low + span)
    masked = jnp.where(own, images, jnp.zeros_like(images)).astype(jnp.float32)

    padded = jnp.pad(psf, ((0, 0), (0, 0), (0, LANES - taps)))
    shape = functools.partial(jax.ShapeDtypeStruct, dtype=jnp.float32)
    table_x, table_y, table_z = pl.pallas_call(
        functools.partial(table_kernel, taps, halo),
        out_shape=[
            shape((group, cells_x, cells_x + 2 * halo)),
            shape((group, cells_y, cells_y + 2 * halo)),
            shape((group, depth, depth)),
        ],
        in_specs=[VMEM],
        out_specs=[VMEM] * 3,
    )(padded)

    start = lax.optimization_barrier(start)
    joined = estimate
    for step in range(ITERS):
        wide = start
        if step > 0:
            wide = gather_halo(joined.astype(jnp.bfloat16), "fy", 1, halo)
            wide = gather_halo(wide, "fx", 0, halo)
        wide = wide.astype(jnp.float32)
        field = jnp.einsum("gox,xyz->goyz", table_x, wide, precision=exact)
        field = jnp.einsum("goy,gxyz->gxoz", table_y, field, precision=exact)
        blurred = jnp.einsum("goz,gxyz->gxyo", table_z, field, precision=exact)
        ratio = masked / blurred
        field = jnp.einsum("goz,gxyo->gxyz", table_z, ratio, precision=exact)
        field = jnp.einsum("goy,gxoz->gxyz", table_y, field, precision=exact)
        field = jnp.einsum("gox,goyz->xyz", table_x, field, precision=exact)
        late = (psf, cover_lo, cover_len) if step == 0 else ()
        below, above, late = swap_fixed(field[:halo], field[cells_x + halo :], "fx", late)
        if step == 0:
            lower_part = weight_of(*view_tables(*late, swap), cells_x, cells_y, depth) + 0.5
        field = add_edges(field[halo : cells_x + halo], below, above, 0)
        below, above, _ = swap_fixed(field[:, :halo], field[:, cells_y + halo :], "fy")
        field = add_edges(field[:, halo : cells_y + halo], below, above, 1)
        moving = pack_fixed(field)
        correction = unpack_fixed(moving)
        for _ in range(groups - 1):
            moving = lax.ppermute(moving, "view", swap)
            correction = correction + unpack_fixed(moving)
        joined = joined * (correction + 0.5) / lower_part
    return joined


def solution(mesh):
    return jax.shard_map(
        body,
        mesh=mesh,
        in_specs=(
            P("fx", "fy", None),
            P("view", "fx", "fy", None),
            P("view", None, None),
            P("view", None, None),
            P("view", None, None),
        ),
        out_specs=P("fx", "fy", None),
        check_vma=False,
    )
```
